256 devices in a mesh: dp: 16 (over z_lo, x, core), seq: 16 (over z_hi, y).
Axes of the slice: x: 4, y: 4, z: 8 (z_hi: 4, z_lo: 2; z = z_hi * 2 + z_lo), core: 2. Of those that a mesh axis runs over, the one named last changes fastest.
Arguments:
- features: bfloat16 [16, 2048, 1024], P('dp', 'seq'), may hold values from -11 to 11
- labels: int32 [16, 2048], P('dp', 'seq'), may hold values from 0 to 172
- label_table: bfloat16 [173, 1024], replicated, may hold values from -3 to 3
- proj_weight: bfloat16 [1024, 4, 1024], P('seq'), may hold values from -0.1875 to 0.1875
- block_order: int32 [16, 16], P('dp'), may hold values from 0 to 15, as said below
- neighbours: int32 [16, 16, 4], P('dp'), may hold values from 0 to 15, as said below
- counts: int32 [16, 16], P('dp'), may hold values from 1 to 4, as said below
- cotangent: bfloat16 [16, 2048, 1024], P('dp', 'seq'), may hold values from -6 to 6
Outputs:
- layer_out: bfloat16 [16, 2048, 1024], P('dp', 'seq')
- features_grad: bfloat16 [16, 2048, 1024], P('dp', 'seq')
- proj_grad: float32 [1024, 4, 1024], P('seq')
The draws below stay inside these ranges and needn't reach their ends.
Inputs may be any that keep to these rules, and one draw needn't show every extreme that they name: `block_order`: each subgraph's row is a permutation of the cluster ids. `neighbours`: slot 0 of stored block s names block_order[s] itself; slot j names block_order[s] + j * t modulo 16 for an odd step t of the row. `counts`: stored block 0 of every subgraph uses all 4 slots.
All inputs are finite; a program needn't handle non-finite values.
Results may differ from the reference program's by a relative error of at most 0.025.
Values may be sent and summed in bfloat16 or wider, within the bound.
A program may use at most 128 MiB of HBM per device.

```python
import math
import jax
import jax.numpy as jnp
from jax import lax

D = 1024
HEADS = 16
HEAD_DIM = 64
BLOCK = 128
NEIGH = 4
NODE_DEV = 128
NODES = 2048
BLOCKS = 16
BATCHES = 16
LABEL_ROWS = 173
N_SEQ = 16


def common_order(key):
    keys = jax.random.split(key, BATCHES)
    return jax.vmap(lambda single: jax.random.permutation(single, BLOCKS))(keys).astype(jnp.int32)


def draw_block_order(key, part):
    return common_order(key)


def draw_neighbours(key, part):
    order = common_order(key)
    key = jax.random.fold_in(key, 7)
    stride = 2 * jax.random.randint(key, (BATCHES, BLOCKS, 1), 0, 4) + 1
    offsets = jnp.arange(NEIGH, dtype=jnp.int32)[None, None, :]
    return ((order[:, :, None] + offsets * stride) % BLOCKS).astype(jnp.int32)


def draw_counts(key, part):
    key = jax.random.fold_in(key, 13)
    first, second = jax.random.split(key)
    one = jax.random.randint(first, (BATCHES, BLOCKS), 0, NEIGH)
    two = jax.random.randint(second, (BATCHES, BLOCKS), 0, NEIGH)
    amount = 1 + jnp.maximum(one, two)
    place = jnp.arange(BLOCKS, dtype=jnp.int32)[None, :]
    return jnp.where(place == 0, NEIGH, amount).astype(jnp.int32)


def draw_features(key, part):
    key = jax.random.fold_in(key, 3)
    first = jax.random.fold_in(key, 0)
    shape = (BATCHES, NODES, D)
    values = jnp.clip(jax.random.normal(first, shape, jnp.float32), -6.0, 6.0)
    return values.astype(jnp.bfloat16)


def draw_proj_weight(key, part):
    key = jax.random.fold_in(key, 5)
    shape = (D, 4, D)
    values = jnp.clip(jax.random.normal(key, shape, jnp.float32), -6.0, 6.0) * D ** (-0.5)
    return values.astype(jnp.bfloat16)


def place_ends(entries, rng, least, largest):
    shape = entries.shape
    spot = [jax.random.randint(jax.random.fold_in(rng, axis), (), 0, shape[axis]) for axis in range(len(shape))]
    entries = entries.at[tuple(spot)].set(least)
    longest = shape.index(max(shape))
    spot[longest] = (spot[longest] + 1) % shape[longest]
    return entries.at[tuple(spot)].set(largest)


def steps_of(key, extent, cuts, smallest, high):
    def one(position, blocks):
        steps = jax.random.uniform(jax.random.fold_in(jax.random.fold_in(key, 6), position), (blocks,), jnp.float32, smallest / len(cuts), high / len(cuts))
        return jnp.repeat(jnp.exp(steps), extent[position] // blocks).reshape((-1,) + (1,) * (len(extent) - position - 1))

    factor_of = one(*cuts[0])
    for cut in cuts[1:]:
        factor_of = factor_of * one(*cut)
    return factor_of


def bell_draw(own_key, dims, scale, most, shards=(), kind=jnp.bfloat16):
    values = jax.random.normal(own_key, dims, jnp.float32) * scale
    if len(shards) > 0:
        values = steps_of(own_key, dims, shards, -0.22, 0.18) * values
    return jnp.clip(values, min=-most, max=most).astype(kind)


def setup_inputs(seed: int = 0) -> dict:
    arg_keys = jax.random.split(jax.random.key(seed), 9)
    features = draw_features(jax.random.fold_in(arg_keys[8], 71), 0)
    labels = place_ends(jax.random.randint(arg_keys[1], (BATCHES, NODES), 0, LABEL_ROWS), jax.random.fold_in(arg_keys[1], 1), 0, LABEL_ROWS - 1).astype(jnp.int32)
    label_table = bell_draw(arg_keys[2], (LABEL_ROWS, D), 0.5, 3.0)
    proj_weight = draw_proj_weight(jax.random.fold_in(arg_keys[8], 71), 0)
    block_order = draw_block_order(jax.random.fold_in(arg_keys[8], 71), 0)
    neighbours = draw_neighbours(jax.random.fold_in(arg_keys[8], 71), 0)
    counts = draw_counts(jax.random.fold_in(arg_keys[8], 71), 0)
    cotangent = bell_draw(arg_keys[7], (BATCHES, NODES, D), 1.0, 6.0, ((0, 16), (1, 16)))
    return dict(features=features, labels=labels, label_table=label_table, proj_weight=proj_weight, block_order=block_order, neighbours=neighbours, counts=counts, cotangent=cotangent)


def lowered(value):
    return lax.optimization_barrier(value.astype(jnp.bfloat16)).astype(jnp.float32)

def slot_tables(order, neigh, cnt):
    positions = jnp.arange(BLOCKS, dtype=jnp.int32)
    slot_of = lax.optimization_barrier(jnp.sum(jnp.where(order[None, :] == positions[:, None], positions[None, :], 0), axis=1)).astype(jnp.int32)
    key_slots = lax.optimization_barrier(jnp.sum(jnp.where(neigh[:, :, None] == positions[None, None, :], slot_of[None, None, :], 0), axis=2)).astype(jnp.int32)
    valid = jnp.arange(NEIGH, dtype=jnp.int32)[None, :] < cnt[:, None]
    return (key_slots, valid)

def block_probs(query, keys, valid):
    scores = jnp.einsum('bqhe,bjkhe->bhqjk', query.astype(jnp.float32), keys.astype(jnp.float32)) / math.sqrt(HEAD_DIM)
    live = valid[:, None, None, :, None]
    top = lax.optimization_barrier(jnp.max(jnp.where(live, scores, -1e+30), axis=(3, 4), keepdims=True))
    expo = jnp.where(live, jnp.exp(scores - top), 0.0)
    return expo / lax.optimization_barrier(jnp.sum(expo, axis=(3, 4), keepdims=True))

def one_graph(feat, lab, order, neigh, cnt, cot, label_table, in_proj, out_proj):
    onehot = (lab[:, None] == jnp.arange(LABEL_ROWS, dtype=jnp.int32)[None, :]).astype(jnp.bfloat16)
    hidden = (feat.astype(jnp.float32) + jnp.dot(onehot, label_table, preferred_element_type=jnp.float32)).astype(jnp.bfloat16)
    qkv = jnp.dot(hidden, in_proj, preferred_element_type=jnp.float32).astype(jnp.bfloat16)
    split = qkv.reshape(BLOCKS, BLOCK, 3, HEADS, HEAD_DIM)
    query, keyset, valueset = (split[:, :, 0], split[:, :, 1], split[:, :, 2])
    key_slots, valid = slot_tables(order, neigh, cnt)
    keys = keyset[key_slots]
    vals = valueset[key_slots]
    probs = block_probs(query, keys, valid)
    probs_low = lowered(probs)
    attn = jnp.einsum('bhqjk,bjkhe->bqhe', probs_low, vals.astype(jnp.float32)).astype(jnp.bfloat16).reshape(NODES, D)
    layer_out = (hidden.astype(jnp.float32) + jnp.dot(attn, out_proj, preferred_element_type=jnp.float32)).astype(jnp.bfloat16)
    grad_attn = jnp.dot(cot, out_proj.T, preferred_element_type=jnp.float32).astype(jnp.bfloat16)
    grad_o = grad_attn.reshape(BLOCKS, BLOCK, HEADS, HEAD_DIM).astype(jnp.float32)
    grad_p = jnp.einsum('bqhe,bjkhe->bhqjk', grad_o, vals.astype(jnp.float32))
    delta = lax.optimization_barrier(jnp.sum(probs * grad_p, axis=(3, 4), keepdims=True))
    grad_s = lowered(probs * (grad_p - delta) / math.sqrt(HEAD_DIM))
    grad_q = jnp.einsum('bhqjk,bjkhe->bqhe', grad_s, keys.astype(jnp.float32)).astype(jnp.bfloat16)
    key_part = jnp.einsum('bhqjk,bqhe->bjkhe', grad_s, query.astype(jnp.float32))
    value_part = jnp.einsum('bhqjk,bqhe->bjkhe', probs_low, grad_o)
    flat_slots = key_slots.reshape(-1)
    grad_k = jax.ops.segment_sum(key_part.reshape(BLOCKS * NEIGH, BLOCK, HEADS, HEAD_DIM), flat_slots, num_segments=BLOCKS).astype(jnp.bfloat16)
    grad_v = jax.ops.segment_sum(value_part.reshape(BLOCKS * NEIGH, BLOCK, HEADS, HEAD_DIM), flat_slots, num_segments=BLOCKS).astype(jnp.bfloat16)
    grad_qkv = jnp.stack([grad_q, grad_k, grad_v], axis=2).reshape(NODES, 3 * D)
    features_grad = (jnp.dot(grad_qkv, in_proj.T, preferred_element_type=jnp.float32) + cot.astype(jnp.float32)).astype(jnp.bfloat16)

    def shard_term(total, pieces):
        hid, gqkv, att, cop = pieces
        term_in = jnp.dot(hid.T, gqkv, preferred_element_type=jnp.float32).reshape(D, 3, D)
        term_out = jnp.dot(att.T, cop, preferred_element_type=jnp.float32)[:, None, :]
        return (total + lowered(jnp.concatenate([term_in, term_out], axis=1)), None)
    pieces = (hidden.reshape(N_SEQ, NODE_DEV, D), grad_qkv.reshape(N_SEQ, NODE_DEV, 3 * D), attn.reshape(N_SEQ, NODE_DEV, D), cot.reshape(N_SEQ, NODE_DEV, D))
    grads, unused = lax.scan(shard_term, jnp.zeros((D, 4, D), jnp.float32), pieces)
    return (layer_out, features_grad, grads)

def reference(features, labels, label_table, proj_weight, block_order, neighbours, counts, cotangent):
    in_proj = proj_weight[:, :3].reshape(D, 3 * D)
    out_proj = proj_weight[:, 3]

    def step(total, pieces):
        feat, lab, order, neigh, cnt, cot = pieces
        layer_out, features_grad, grads = one_graph(feat, lab, order, neigh, cnt, cot, label_table, in_proj, out_proj)
        return (total + grads, (layer_out, features_grad))
    proj_grad, outs = lax.scan(step, jnp.zeros((D, 4, D), jnp.float32), (features, labels, block_order, neighbours, counts, cotangent))
    return (outs[0], outs[1], proj_grad)
```

```python
import jax
import jax.numpy as jnp
from jax import lax
from jax.experimental import pallas as pl
from jax.experimental.pallas import tpu as pltpu
from jax.sharding import PartitionSpec as P

XS, YS, TEAM, SEQ, ROWS, WIDTH = 4, 4, 8, 16, 128, 1024
SHARD = WIDTH // SEQ
BF, F32 = jnp.bfloat16, jnp.float32
NN = (((1,), (0,)), ((), ()))
NT = (((1,), (1,)), ((), ()))
TN = (((0,), (0,)), ((), ()))
VMEM_BYTES = 48 << 20


def dot(a, b, dims=NN):
    return lax.dot_general(a, b, dims, preferred_element_type=F32)


def place():
    dp, seq = lax.axis_index("dp"), lax.axis_index("seq")
    return dp // TEAM, dp % TEAM, seq


def push(src, dst, send, recv, dp, seq):
    copy = pltpu.make_async_remote_copy(
        src_ref=src,
        dst_ref=dst,
        send_sem=send,
        recv_sem=recv,
        device_id=(dp, seq),
        device_id_type=pl.DeviceIdType.MESH,
    )
    copy.start()
    return copy


def await_recv(dst, recv, dp, seq):
    pltpu.make_async_remote_copy(
        src_ref=dst,
        dst_ref=dst,
        send_sem=recv,
        recv_sem=recv,
        device_id=(dp, seq),
        device_id_type=pl.DeviceIdType.MESH,
    ).wait_recv()


def greet(peers):
    barrier = pltpu.get_barrier_semaphore()
    for dp, seq in peers:
        pl.semaphore_signal(
            barrier, inc=1, device_id=(dp, seq), device_id_type=pl.DeviceIdType.MESH
        )
    pl.semaphore_wait(barrier, len(peers))


def low_lanes(shape):
    return lax.broadcasted_iota(jnp.int32, shape, 1) < 64


def merge(a, b):
    return jnp.where(low_lanes(a.shape), a, pltpu.roll(b, 64, 1))


def merge_high(a, b):
    return jnp.where(low_lanes(a.shape), pltpu.roll(a, 64, 1), b)


def gather_kernel(
    hid, cot, wt, tab,
    qg_out, hid8_out, cot8_out, wg_out, tab_out,
    hid8, cot8, wg, wo, tab8, vals, stage, land,
    hid_s, hid_r, cot_s, cot_r, tab_s, tab_r, w_s, w_r, o_s, o_r, sc_s, sc_r, a_s, a_r, loc,
):
    zl, p, r = place()
    x, c = p // 2, p % 2
    zh, y = r // YS, r % YS
    base = zl * TEAM
    dp = base + p

    def team(dx, dc):
        return lax.rem(x + dx, XS) * 2 + lax.rem(c + dc, 2)

    def at_z(k):
        return lax.rem(zh + k, 4) * YS + y

    def at_y(k):
        return zh * YS + lax.rem(y + k, YS)

    greet(
        [(base + lax.rem(p + k, TEAM), r) for k in range(1, TEAM)]
        + [(dp, lax.rem(r + k, SEQ)) for k in range(1, SEQ)]
    )
    sends = []

    def rows_of(s):
        return pl.ds(pl.multiple_of(s * SHARD, SHARD), SHARD)

    def in_part(s):
        return wg.at[rows_of(s), 0:384]

    def out_part(s):
        return wg.at[rows_of(s), 384:512]

    own = pltpu.make_async_copy(wt.at[p, :, 0:384], in_part(r), loc.at[0])
    own.start()
    for k in (1, 3, 2):
        sends.append(
            push(wt.at[p, :, 0:384], in_part(r), w_s.at[k], w_r.at[r], dp, at_z(k))
        )
    for k in (1, 3, 2):
        sends.append(
            push(wt.at[p, :, 0:384], in_part(r), w_s.at[3 + k], w_r.at[r], dp, at_y(k))
        )

    mine = r // 2 == p

    @pl.when(mine)
    def _():
        for j in range(TEAM):
            t = 2 * j + r % 2

            @pl.when(t != r)
            def _():
                push(wt.at[j, :, 384:512], out_part(t), sc_s.at[j], sc_r, dp, t)

    keep_hid = pltpu.make_async_copy(hid, hid8.at[p], loc.at[1])
    keep_hid.start()
    keep_cot = pltpu.make_async_copy(cot, cot8.at[p], loc.at[2])
    keep_cot.start()
    for k, (dx, dc) in enumerate(((1, 0), (3, 0), (2, 0), (0, 1))):
        sends.append(
            push(hid, hid8.at[p], hid_s.at[k], hid_r.at[p], base + team(dx, dc), r)
        )
    for k in range(1, TEAM):
        sends.append(
            push(tab, tab8.at[p], tab_s.at[k], tab_r.at[p], base + lax.rem(p + k, TEAM), r)
        )

    for n, k in enumerate((1, 3, 2)):
        s = at_z(k)
        await_recv(in_part(s), w_r.at[s], dp, s)
        for m in (1, 3, 2):
            sends.append(
                push(in_part(s), in_part(s), w_s.at[7 + n * 3 + m], w_r.at[s], dp, at_y(m))
            )

    piece = out_part(r)

    @pl.when(mine)
    def _():
        copy = pltpu.make_async_copy(wt.at[p, :, 384:512], piece, loc.at[3])
        copy.start()
        copy.wait()

    @pl.when(jnp.logical_not(mine))
    def _():
        await_recv(piece, sc_r, dp, r)

    for k in (1, 3, 2):
        sends.append(push(piece, piece, o_s.at[k], o_r.at[r], dp, at_z(k)))
    for k in (1, 3, 2):
        sends.append(push(piece, piece, o_s.at[3 + k], o_r.at[r], dp, at_y(k)))

    for n, dx in enumerate((1, 3, 2)):
        i = team(dx, 0)
        await_recv(hid8.at[i], hid_r.at[i], base + i, r)
        sends.append(
            push(hid8.at[i], hid8.at[i], hid_s.at[4 + n], hid_r.at[i], base + team(0, 1), r)
        )
    for k, (dx, dc) in enumerate(((1, 0), (3, 0), (2, 0), (0, 1))):
        sends.append(
            push(cot, cot8.at[p], cot_s.at[k], cot_r.at[p], base + team(dx, dc), r)
        )
    for n, k in enumerate((1, 3, 2)):
        s = at_z(k)
        await_recv(out_part(s), o_r.at[s], dp, s)
        for m in (1, 3, 2):
            sends.append(
                push(out_part(s), out_part(s), o_s.at[7 + n * 3 + m], o_r.at[s], dp, at_y(m))
            )

    for m in (1, 3, 2):
        for k in range(4):
            s = lax.rem(zh + k, 4) * YS + lax.rem(y + m, YS)
            await_recv(in_part(s), w_r.at[s], dp, s)
    own.wait()
    keep_hid.wait()

    def deliver(i, e, half):
        t = 2 * i + e

        @pl.when(t != r)
        def _():
            push(
                stage.at[t, half], land.at[r, half], a_s.at[t, half], a_r.at[r, half], dp, t
            )

        @pl.when(t == r)
        def _():
            land[r, half] = stage[t, half]

    order = ((0, 0), (0, 1), (1, 0), (3, 0), (1, 1), (3, 1), (2, 0), (2, 1))
    for dx, dc in order:
        i = team(dx, dc)
        if dc == 1:
            await_recv(hid8.at[i], hid_r.at[i], base + i, r)
        qkv = dot(hid8[i], wg[:, 0:384]).astype(BF)
        q, k, v = qkv[:, 0:128], qkv[:, 128:256], qkv[:, 256:384]
        vals[i] = v
        stage[2 * i, 0] = merge(q, k)
        stage[2 * i + 1, 0] = merge_high(q, k)
        deliver(i, 0, 0)
        deliver(i, 1, 0)

    keep_cot.wait()
    for n, dx in enumerate((1, 3, 2)):
        i = team(dx, 0)
        await_recv(cot8.at[i], cot_r.at[i], base + i, r)
        sends.append(
            push(cot8.at[i], cot8.at[i], cot_s.at[4 + n], cot_r.at[i], base + team(0, 1), r)
        )
    for m in (1, 3, 2):
        for k in range(4):
            s = lax.rem(zh + k, 4) * YS + lax.rem(y + m, YS)
            await_recv(out_part(s), o_r.at[s], dp, s)
    for j in range(TEAM):
        wo[128 * j : 128 * j + 128, :] = wg[128 * j : 128 * j + 128, 384:512].T
    for dx, dc in order:
        i = team(dx, dc)
        if dc == 1:
            await_recv(cot8.at[i], cot_r.at[i], base + i, r)
        g = dot(cot8[i], wo[...]).astype(BF)
        v = vals[i]
        stage[2 * i, 1] = merge(v, g)
        stage[2 * i + 1, 1] = merge_high(v, g)
        deliver(i, 0, 1)
        deliver(i, 1, 1)

    for copy in sends:
        copy.wait_send()
    wg[:, 384:512] = wo[...]
    outs = [
        pltpu.make_async_copy(hid8, hid8_out, loc.at[0]),
        pltpu.make_async_copy(cot8, cot8_out, loc.at[1]),
        pltpu.make_async_copy(wg, wg_out, loc.at[2]),
    ]
    for copy in outs:
        copy.start()
    for k in range(1, TEAM):
        i = lax.rem(p + k, TEAM)
        await_recv(tab8.at[i], tab_r.at[i], base + i, r)
    tab8[p] = tab[...]
    tab_out[...] = tab8[r // 2]

    @pl.when(mine)
    def _():
        for j in range(TEAM):
            t = 2 * j + r % 2

            @pl.when(t != r)
            def _():
                pltpu.make_async_remote_copy(
                    src_ref=wt.at[j, :, 384:512],
                    dst_ref=out_part(t),
                    send_sem=sc_s.at[j],
                    recv_sem=sc_r,
                    device_id=(dp, t),
                    device_id_type=pl.DeviceIdType.MESH,
                ).wait_send()

    for k in range(1, SEQ):
        t = lax.rem(r + k, SEQ)
        for half in (0, 1):
            await_recv(land.at[t, half], a_r.at[t, half], dp, t)
            pltpu.make_async_remote_copy(
                src_ref=stage.at[t, half],
                dst_ref=land.at[r, half],
                send_sem=a_s.at[t, half],
                recv_sem=a_r.at[r, half],
                device_id=(dp, t),
                device_id_type=pl.DeviceIdType.MESH,
            ).wait_send()
    last = pltpu.make_async_copy(land, qg_out, loc.at[3])
    last.start()
    for copy in outs:
        copy.wait()
    last.wait()


def gather(hid, cot, wt, tab):
    any_ = pl.BlockSpec(memory_space=pl.ANY)
    vmem = pl.BlockSpec(memory_space=pltpu.VMEM)
    dma = pltpu.SemaphoreType.DMA
    shapes = [
        ((SEQ, 2, 128, 128), BF),
        ((TEAM, ROWS, WIDTH), BF),
        ((TEAM, ROWS, WIDTH), BF),
        ((WIDTH, 512), BF),
        ((8, 128), jnp.int32),
    ]
    return pl.pallas_call(
        gather_kernel,
        out_shape=[jax.ShapeDtypeStruct(s, d) for s, d in shapes],
        in_specs=[vmem] * 4,
        out_specs=[any_] * 4 + [vmem],
        scratch_shapes=[
            pltpu.VMEM((TEAM, ROWS, WIDTH), BF),
            pltpu.VMEM((TEAM, ROWS, WIDTH), BF),
            pltpu.VMEM((WIDTH, 512), BF),
            pltpu.VMEM((WIDTH, 128), BF),
            pltpu.VMEM((TEAM, 8, 128), jnp.int32),
            pltpu.VMEM((TEAM, 128, 128), BF),
            pltpu.VMEM((SEQ, 2, 128, 128), BF),
            pltpu.VMEM((SEQ, 2, 128, 128), BF),
            dma((8,)), dma((8,)), dma((8,)), dma((8,)), dma((8,)), dma((8,)),
            dma((17,)), dma((16,)), dma((17,)), dma((16,)), dma((8,)), dma(()),
            dma((16, 2)), dma((16, 2)), dma((4,)),
        ],
        compiler_params=pltpu.CompilerParams(
            collective_id=1, has_side_effects=True, vmem_limit_bytes=VMEM_BYTES
        ),
    )(hid, cot, wt, tab)


def attend_kernel(tab, a, out, acc, slot_of):
    for s in range(SEQ):
        slot_of[tab[0, s]] = s
    acc[...] = jnp.zeros_like(acc)
    lo = low_lanes((128, 128))
    zero = jnp.zeros((128, 128), BF)

    def step(s, carry):
        qk, vg = a[s, 0], a[s, 1]
        qz = jnp.where(lo, zero, pltpu.roll(qk, 64, 1)) * jnp.asarray(0.125, BF)
        gz = jnp.where(lo, pltpu.roll(vg, 64, 1), zero)
        rhs = jnp.concatenate([jnp.where(lo, qk, zero), jnp.where(lo, zero, vg)], axis=0)
        count = tab[0, 80 + s]
        slots = [slot_of[tab[0, 16 + 4 * s + j]] for j in range(4)]
        keys = [a[b, 0] for b in slots]
        vals = [a[b, 1] for b in slots]
        scores = [
            jnp.where(j < count, dot(k, qz, NT), -1e30) for j, k in enumerate(keys)
        ]
        grad_p = [dot(v, gz, NT) for v in vals]
        top = jnp.max(
            jnp.maximum(jnp.maximum(scores[0], scores[1]), jnp.maximum(scores[2], scores[3])),
            axis=0,
            keepdims=True,
        )
        expo = [jnp.exp(v - top) for v in scores]
        total = jnp.sum((expo[0] + expo[1]) + (expo[2] + expo[3]), axis=0, keepdims=True)
        inv = 1.0 / total
        probs = [e * inv for e in expo]
        prod = [p * g for p, g in zip(probs, grad_p)]
        delta = jnp.sum((prod[0] + prod[1]) + (prod[2] + prod[3]), axis=0, keepdims=True)
        low = [p.astype(BF) for p in probs]
        grad_s = [
            (p * (g - delta) * 0.125).astype(BF) for p, g in zip(probs, grad_p)
        ]
        attn = dot(jnp.concatenate(low, axis=0), jnp.concatenate(vals, axis=0), TN)
        grad_q = dot(jnp.concatenate(grad_s, axis=0), jnp.concatenate(keys, axis=0), TN)
        out[s, 0] = jnp.where(lo, attn, grad_q).astype(BF)
        for j in range(4):
            acc[slots[j]] += dot(jnp.concatenate([grad_s[j], low[j]], axis=1), rhs)
        return carry

    lax.fori_loop(0, SEQ, step, 0)
    for s in range(SEQ):
        out[s, 1] = acc[s].astype(BF)


def attend(tab, a):
    vmem = pl.BlockSpec(memory_space=pltpu.VMEM)
    return pl.pallas_call(
        attend_kernel,
        out_shape=jax.ShapeDtypeStruct((SEQ, 2, 128, 128), BF),
        in_specs=[pl.BlockSpec(memory_space=pltpu.SMEM), vmem],
        out_specs=vmem,
        scratch_shapes=[pltpu.VMEM((SEQ, 128, 128), F32), pltpu.SMEM((SEQ,), jnp.int32)],
        compiler_params=pltpu.CompilerParams(vmem_limit_bytes=VMEM_BYTES),
    )(tab, a)


def finish_kernel(
    ao, hid8_in, cot8_in, wg_in,
    layer_out, features_grad, proj_grad,
    hid8, cot8, wg, land, mix, part, sib, far, terms, from_y, to_z, from_z, from_zl, full, wob,
    a_s, a_r, sib_s, sib_r, far_s, far_r, y_s, y_r, z_s, z_r, zl_s, zl_r, g_s, g_r, o_s, o_r, loc,
):
    zl, p, r = place()
    x, c = p // 2, p % 2
    zh, y = r // YS, r % YS
    base = zl * TEAM
    dp = base + p
    other = lax.rem(dp + TEAM, 2 * TEAM)

    def team(dx, dc):
        return lax.rem(x + dx, XS) * 2 + lax.rem(c + dc, 2)

    loads = [
        pltpu.make_async_copy(wg_in, wg, loc.at[0]),
        pltpu.make_async_copy(hid8_in, hid8, loc.at[1]),
        pltpu.make_async_copy(cot8_in, cot8, loc.at[2]),
    ]
    for copy in loads:
        copy.start()
    greet(
        [(base + lax.rem(p + k, TEAM), r) for k in range(1, TEAM)]
        + [(dp, lax.rem(r + k, SEQ)) for k in range(1, SEQ)]
        + [(other, r)]
    )
    sends = []
    for k in range(1, SEQ):
        t = lax.rem(r + k, SEQ)
        sends.append(push(ao.at[t], land.at[r], a_s.at[k], a_r.at[r], dp, t))
    land[r] = ao[r]
    for copy in loads:
        copy.wait()

    def arrive(t):
        @pl.when(t != r)
        def _():
            await_recv(land.at[t], a_r.at[t], dp, t)

    def work(i):
        arrive(2 * i)
        arrive(2 * i + 1)
        a0, a1 = land[2 * i, 0], land[2 * i + 1, 0]
        b0, b1 = land[2 * i, 1], land[2 * i + 1, 1]
        attn = merge(a0, a1)
        grads = jnp.concatenate([merge_high(a0, a1), merge(b0, b1), merge_high(b0, b1)], axis=1)
        rows = pl.ds(pl.multiple_of(i * ROWS, ROWS), ROWS)
        mix[rows, 0:128] = attn
        mix[rows, 128:512] = grads
        return dot(attn, wg[:, 384:512], NT), dot(grads, wg[:, 0:384], NT)

    for n, dx in enumerate((1, 3, 2, 0)):
        lo, fg = work(team(dx, 1))
        part[n, 0] = lo.astype(BF)
        part[n, 1] = fg.astype(BF)
        sends.append(
            push(part.at[n], sib.at[n], sib_s.at[n], sib_r.at[n], base + team(0, 1), r)
        )
    for n, dx in enumerate((1, 3, 2, 0)):
        i = team(dx, 0)
        lo, fg = work(i)
        await_recv(sib.at[n], sib_r.at[n], base + team(0, 1), r)
        lo += sib[n, 0].astype(F32)
        fg += sib[n, 1].astype(F32)
        if dx:
            part[4 + n, 0] = lo.astype(BF)
            part[4 + n, 1] = fg.astype(BF)
            sends.append(
                push(part.at[4 + n], far.at[n], far_s.at[n], far_r.at[n], base + i, r)
            )

    out_term = dot(mix[:, 0:128], cot8[...].reshape(TEAM * ROWS, WIDTH), TN)
    for j in range(TEAM):
        block = out_term[:, 128 * j : 128 * j + 128].astype(BF)
        terms[2 * j, :, 384:512] = block[0:64]
        terms[2 * j + 1, :, 384:512] = block[64:128]
    for h in range(4):
        hidden = hid8[:, :, 256 * h : 256 * h + 256].reshape(TEAM * ROWS, 256)
        in_term = dot(hidden, mix[:, 128:512], TN)
        for m in range(YS):
            terms[4 * h + m, :, 0:384] = in_term[64 * m : 64 * m + 64].astype(BF)
        for k in (1, 3, 2):
            t = lax.rem(y + k, YS)
            sends.append(
                push(
                    terms.at[4 * h + t], from_y.at[y, h], y_s.at[k, h], y_r.at[y, h],
                    dp, zh * YS + t,
                )
            )

    for n in range(3):
        await_recv(far.at[n], far_r.at[n], dp, r)
        lo += far[n, 0].astype(F32)
        fg += far[n, 1].astype(F32)
    layer_out[...] = (hid8[p].astype(F32) + lo).astype(BF)
    features_grad[...] = (cot8[p].astype(F32) + fg).astype(BF)

    for k in (1, 2, 3, 0):
        h = lax.rem(zh + k, 4)
        total = terms[4 * h + y].astype(F32)
        for m in (1, 3, 2):
            t = lax.rem(y + m, YS)
            await_recv(from_y.at[t, h], y_r.at[t, h], dp, r)
            total += from_y[t, h].astype(F32)
        if k:
            to_z[h] = total.astype(BF)
            sends.append(
                push(to_z.at[h], from_z.at[zh], z_s.at[h], z_r.at[zh], dp, h * YS + y)
            )
    for k in (1, 3, 2):
        h = lax.rem(zh + k, 4)
        await_recv(from_z.at[h], z_r.at[h], dp, r)
        total += from_z[h].astype(F32)
    to_z[zh] = total.astype(BF)
    sends.append(push(to_z.at[zh], from_zl, zl_s, zl_r, other, r))
    await_recv(from_zl, zl_r, other, r)
    full[p] = (to_z[zh].astype(F32) + from_zl[...].astype(F32)).astype(BF)

    for k in range(1, TEAM):
        i = lax.rem(p + k, TEAM)
        sends.append(push(full.at[p], full.at[p], g_s.at[k], g_r.at[p], base + i, r))
    for k in range(TEAM):
        i = lax.rem(p + k, TEAM)
        if k:
            await_recv(full.at[i], g_r.at[i], base + i, r)
        t = 2 * i + r % 2

        @pl.when(t != r)
        def _():
            push(full.at[i, :, 384:512], wob.at[r // 2], o_s.at[i], o_r.at[r // 2], dp, t)

        @pl.when(t == r)
        def _():
            wob[r // 2] = full[i, :, 384:512]

    for i in range(TEAM):
        for n in range(3):
            proj_grad[n, :, 128 * i : 128 * i + 128] = full[
                i, :, 128 * n : 128 * n + 128
            ].astype(F32)
    for j in range(TEAM):
        t = 2 * j + r % 2

        @pl.when(t != r)
        def _():
            await_recv(wob.at[j], o_r.at[j], dp, t)
            pltpu.make_async_remote_copy(
                src_ref=full.at[j, :, 384:512],
                dst_ref=wob.at[r // 2],
                send_sem=o_s.at[j],
                recv_sem=o_r.at[r // 2],
                device_id=(dp, t),
                device_id_type=pl.DeviceIdType.MESH,
            ).wait_send()

        proj_grad[3, :, 128 * j : 128 * j + 128] = wob[j].astype(F32)
    for copy in sends:
        copy.wait_send()


def finish(ao, hid8, cot8, wg):
    any_ = pl.BlockSpec(memory_space=pl.ANY)
    vmem = pl.BlockSpec(memory_space=pltpu.VMEM)
    dma = pltpu.SemaphoreType.DMA
    return pl.pallas_call(
        finish_kernel,
        out_shape=[
            jax.ShapeDtypeStruct((ROWS, WIDTH), BF),
            jax.ShapeDtypeStruct((ROWS, WIDTH), BF),
            jax.ShapeDtypeStruct((4, SHARD, WIDTH), F32),
        ],
        in_specs=[vmem, any_, any_, any_],
        out_specs=[vmem] * 3,
        scratch_shapes=[
            pltpu.VMEM((TEAM, ROWS, WIDTH), BF),
            pltpu.VMEM((TEAM, ROWS, WIDTH), BF),
            pltpu.VMEM((WIDTH, 512), BF),
            pltpu.VMEM((SEQ, 2, 128, 128), BF),
            pltpu.VMEM((TEAM * ROWS, 512), BF),
            pltpu.VMEM((7, 2, ROWS, WIDTH), BF),
            pltpu.VMEM((4, 2, ROWS, WIDTH), BF),
            pltpu.VMEM((3, 2, ROWS, WIDTH), BF),
            pltpu.VMEM((SEQ, SHARD, 512), BF),
            pltpu.VMEM((4, 4, SHARD, 512), BF),
            pltpu.VMEM((4, SHARD, 512), BF),
            pltpu.VMEM((4, SHARD, 512), BF),
            pltpu.VMEM((SHARD, 512), BF),
            pltpu.VMEM((TEAM, SHARD, 512), BF),
            pltpu.VMEM((TEAM, SHARD, 128), BF),
            dma((16,)), dma((16,)), dma((4,)), dma((4,)), dma((3,)), dma((3,)),
            dma((4, 4)), dma((4, 4)), dma((4,)), dma((4,)), dma(()), dma(()),
            dma((8,)), dma((8,)), dma((8,)), dma((8,)), dma((3,)),
        ],
        compiler_params=pltpu.CompilerParams(
            collective_id=2, has_side_effects=True, vmem_limit_bytes=VMEM_BYTES
        ),
    )(ao, hid8, cot8, wg)


def per_device(
    features, labels, label_table, proj_weight, block_order, neighbours, counts, cotangent
):
    onehot = (labels[0][:, None] == lax.iota(jnp.int32, label_table.shape[0])[None, :]).astype(BF)
    hidden = (
        features[0].astype(F32) + jnp.dot(onehot, label_table, preferred_element_type=F32)
    ).astype(BF)
    wt = proj_weight.reshape(SHARD, 4, TEAM, 128).transpose(2, 0, 1, 3).reshape(TEAM, SHARD, 512)
    tab = jnp.concatenate(
        [
            block_order[0],
            neighbours[0].reshape(-1),
            counts[0],
            jnp.zeros((32,), jnp.int32),
        ]
    )
    tab = jnp.broadcast_to(tab[None, :], (8, 128))
    qg, hid8, cot8, wg, table = gather(hidden, cotangent[0], wt, tab)
    ao = attend(table, qg)
    layer_out, features_grad, proj_grad = finish(ao, hid8, cot8, wg)
    return (layer_out[None], features_grad[None], proj_grad.transpose(1, 0, 2))


def solution(mesh):
    placed = (
        P("dp", "seq", None),
        P("dp", "seq"),
        P(),
        P("seq", None, None),
        P("dp", None),
        P("dp", None, None),
        P("dp", None),
        P("dp", "seq", None),
    )
    return jax.shard_map(
        per_device,
        mesh=mesh,
        in_specs=placed,
        out_specs=(P("dp", "seq", None), P("dp", "seq", None), P("seq", None, None)),
        check_vma=False,
    )
```

```python
import jax
import jax.numpy as jnp
from jax import lax
from jax.experimental import pallas as pl
from jax.experimental.pallas import tpu as pltpu
from jax.sharding import PartitionSpec as P

XS, YS, TEAM, SEQ, ROWS, WIDTH = 4, 4, 8, 16, 128, 1024
SHARD = WIDTH // SEQ
HALF = 4 * ROWS
BF, F32 = jnp.bfloat16, jnp.float32
NN = (((1,), (0,)), ((), ()))
NT = (((1,), (1,)), ((), ()))
TN = (((0,), (0,)), ((), ()))
VMEM_BYTES = 40 << 20
MESH = pl.DeviceIdType.MESH
NEAR = (1, 3, 2)


def dot(a, b, dims=NN):
    return lax.dot_general(a, b, dims, preferred_element_type=F32)


def remote(src, dst, send, recv, where):
    return pltpu.make_async_remote_copy(
        src_ref=src, dst_ref=dst, send_sem=send, recv_sem=recv, device_id=where, device_id_type=MESH
    )


def push(src, dst, send, recv, where):
    copy = remote(src, dst, send, recv, where)
    copy.start()
    return copy


def arrival(dst, recv, where):
    remote(dst, dst, recv, recv, where).wait_recv()


def low_lanes(shape):
    return lax.broadcasted_iota(jnp.int32, shape, 1) < 64


def merge(a, b):
    return jnp.where(low_lanes(a.shape), a, pltpu.roll(b, 64, 1))


def merge_high(a, b):
    return jnp.where(low_lanes(a.shape), pltpu.roll(a, 64, 1), b)


def kernel(
    hid, cot, wt, tab,
    layer_out, features_grad, proj_grad,
    hid8, cot8, hid_t, wg, wo, w_t, tab8, tabs, stage, land_qk, land_vg, probs, tiles, back, home, mix,
    part, sib, far, terms, from_y, to_z, from_z, from_zl, full, wob,
    hid_s, hid_r, cot_s, cot_r, tab_s, tab_r, w_s, w_r, v_s, v_r, o_s, o_r, sc_s, sc_r, a_s, a_r, b_s, b_r,
    sib_s, sib_r, far_s, far_r, y_s, y_r, z_s, z_r, zl_s, zl_r, g_s, g_r, q_s, q_r, loc,
):
    dp, r = lax.axis_index("dp"), lax.axis_index("seq")
    zl, p = dp // TEAM, dp % TEAM
    x, c = p // 2, p % 2
    zh, y = r // YS, r % YS
    base = zl * TEAM
    me = c * XS + x
    sibling = (base + x * 2 + 1 - c, r)
    partner = (lax.rem(dp + TEAM, 2 * TEAM), r)

    def turn(k):
        return lax.rem(x + k, XS)

    def slot(k):
        return c * XS + turn(k)

    def at_x(k):
        return (base + turn(k) * 2 + c, r)

    def at_z(k):
        return lax.rem(zh + k, 4) * YS + y

    def at_y(k):
        return zh * YS + lax.rem(y + k, YS)

    def team_peer(k):
        return base + lax.rem(p + k, TEAM)

    def slot_of(q):
        return lax.rem(q, 2) * XS + q // 2

    barrier = pltpu.get_barrier_semaphore()
    greeted = [(team_peer(k), r) for k in range(1, TEAM)]
    greeted += [(dp, lax.rem(r + k, SEQ)) for k in range(1, SEQ)] + [partner]
    for where in greeted:
        pl.semaphore_signal(barrier, inc=1, device_id=where, device_id_type=MESH)
    pl.semaphore_wait(barrier, len(greeted))
    sends = []
    land = (land_qk, land_vg)

    def rows_of(s):
        return pl.ds(pl.multiple_of(s * SHARD, SHARD), SHARD)

    def qk_part(s):
        return wg.at[rows_of(s), 0:256]

    def v_part(s):
        return wg.at[rows_of(s), 256:384]

    def out_part(s):
        return wg.at[rows_of(s), 384:512]

    own_w = pltpu.make_async_copy(wt.at[p, :, 0:384], wg.at[rows_of(r), 0:384], loc.at[0])
    own_w.start()
    mine_qk, mine_v = wt.at[p, :, 0:256], wt.at[p, :, 256:384]
    for k in NEAR:
        sends.append(push(mine_qk, qk_part(r), w_s.at[k], w_r.at[r], (dp, at_z(k))))
        sends.append(push(mine_v, v_part(r), v_s.at[k], v_r.at[r], (dp, at_y(k))))
    for k in NEAR:
        sends.append(push(mine_qk, qk_part(r), w_s.at[3 + k], w_r.at[r], (dp, at_y(k))))
        sends.append(push(mine_v, v_part(r), v_s.at[3 + k], v_r.at[r], (dp, at_z(k))))

    spread = r // 2 == p

    @pl.when(spread)
    def _():
        for j in range(TEAM):
            t = 2 * j + r % 2

            @pl.when(t != r)
            def _():
                push(wt.at[j, :, 384:512], out_part(t), sc_s.at[j], sc_r, (dp, t))

    keep_hid = pltpu.make_async_copy(hid, hid8.at[me], loc.at[1])
    keep_hid.start()
    keep_cot = pltpu.make_async_copy(cot, cot8.at[me], loc.at[2])
    keep_cot.start()
    for k in NEAR:
        sends.append(push(hid, hid8.at[me], hid_s.at[k], hid_r.at[me], at_x(k)))
    sends.append(push(hid, hid8.at[me], hid_s.at[0], hid_r.at[me], sibling))
    for k in range(1, TEAM):
        sends.append(push(tab, tab8.at[me], tab_s.at[k], tab_r.at[me], (team_peer(k), r)))

    for n, k in enumerate(NEAR):
        s = at_z(k)
        arrival(qk_part(s), w_r.at[s], (dp, s))
        for m in NEAR:
            sends.append(
                push(qk_part(s), qk_part(s), w_s.at[7 + n * 3 + m], w_r.at[s], (dp, at_y(m)))
            )
        s = at_y(k)
        arrival(v_part(s), v_r.at[s], (dp, s))
        for m in NEAR:
            sends.append(
                push(v_part(s), v_part(s), v_s.at[7 + n * 3 + m], v_r.at[s], (dp, at_z(m)))
            )

    piece = out_part(r)

    @pl.when(spread)
    def _():
        copy = pltpu.make_async_copy(wt.at[p, :, 384:512], piece, loc.at[3])
        copy.start()
        copy.wait()

    @pl.when(jnp.logical_not(spread))
    def _():
        arrival(piece, sc_r, (dp, r))

    for k in NEAR:
        sends.append(push(piece, piece, o_s.at[k], o_r.at[r], (dp, at_z(k))))
    for k in NEAR:
        sends.append(push(piece, piece, o_s.at[3 + k], o_r.at[r], (dp, at_y(k))))

    for n, k in enumerate(NEAR):
        q = slot(k)
        arrival(hid8.at[q], hid_r.at[q], at_x(k))
        sends.append(push(hid8.at[q], hid8.at[q], hid_s.at[4 + n], hid_r.at[q], sibling))
    for k in NEAR:
        sends.append(push(cot, cot8.at[me], cot_s.at[k], cot_r.at[me], at_x(k)))
    sends.append(push(cot, cot8.at[me], cot_s.at[0], cot_r.at[me], sibling))
    for n, k in enumerate(NEAR):
        s = at_z(k)
        arrival(out_part(s), o_r.at[s], (dp, s))
        for m in NEAR:
            sends.append(
                push(out_part(s), out_part(s), o_s.at[7 + n * 3 + m], o_r.at[s], (dp, at_y(m)))
            )

    def from_all_y(piece_of, sems):
        for m in NEAR:
            for k in range(4):
                s = lax.rem(zh + k, 4) * YS + lax.rem(y + m, YS)
                arrival(piece_of(s), sems.at[s], (dp, s))

    from_all_y(qk_part, w_r)
    own_w.wait()
    keep_hid.wait()

    def deliver(t, half):
        @pl.when(t != r)
        def _():
            push(
                stage.at[t, half], land[half].at[r], a_s.at[t, half], a_r.at[r, half], (dp, t)
            )

        @pl.when(t == r)
        def _():
            land[half][r] = stage[t, half]

    def group_rows(array, core):
        block = array[pl.ds(pl.multiple_of(core * XS, XS), XS)]
        return block.reshape(HALF, array.shape[2])

    for core in (c, 1 - c):
        if core is not c:
            for k in range(XS):
                q = (1 - c) * XS + turn(k)
                arrival(hid8.at[q], hid_r.at[q], sibling)
        queries_keys = dot(group_rows(hid8, core), wg[:, 0:256]).astype(BF)
        for n in range(XS):
            rows = queries_keys[n * ROWS : n * ROWS + ROWS]
            q, k = rows[:, 0:128], rows[:, 128:256]
            i = core * XS + n
            stage[2 * i, 0] = merge(q, k)
            stage[2 * i + 1, 0] = merge_high(q, k)
            deliver(2 * i, 0)
            deliver(2 * i + 1, 0)

    keep_cot.wait()
    for n, k in enumerate(NEAR):
        q = slot(k)
        arrival(cot8.at[q], cot_r.at[q], at_x(k))
        sends.append(push(cot8.at[q], cot8.at[q], cot_s.at[4 + n], cot_r.at[q], sibling))
    for m in NEAR:
        for k in range(1, 4):
            s = lax.rem(zh + k, 4) * YS + lax.rem(y + m, YS)
            arrival(v_part(s), v_r.at[s], (dp, s))
    for k in NEAR:
        s = at_z(k)
        arrival(v_part(s), v_r.at[s], (dp, s))
    from_all_y(out_part, o_r)
    for j in range(TEAM):
        block = wg[128 * j : 128 * j + 128, 384:512]
        wo[128 * j : 128 * j + 128, :] = block.T
        w_t[384:512, 128 * j : 128 * j + 128] = block
    for core in (c, 1 - c):
        if core is not c:
            for k in range(XS):
                q = (1 - c) * XS + turn(k)
                arrival(cot8.at[q], cot_r.at[q], sibling)
        values = dot(group_rows(hid8, core), wg[:, 256:384]).astype(BF)
        grad = dot(group_rows(cot8, core), wo[...]).astype(BF)
        for n in range(XS):
            g = grad[n * ROWS : n * ROWS + ROWS]
            v = values[n * ROWS : n * ROWS + ROWS]
            i = core * XS + n
            stage[2 * i, 1] = merge(v, g)
            stage[2 * i + 1, 1] = merge_high(v, g)
            deliver(2 * i, 1)
            deliver(2 * i + 1, 1)

    for n in range(3):
        w_t[128 * n : 128 * n + 128, :] = wg[:, 128 * n : 128 * n + 128].T
    for q in range(TEAM):
        hid_t[:, 128 * q : 128 * q + 128] = hid8[q].T

    for k in range(1, TEAM):
        i = lax.rem(p + k, TEAM)
        q = slot_of(i)
        arrival(tab8.at[q], tab_r.at[q], (base + i, r))
    tab8[me] = tab[...]
    to_scalars = pltpu.make_async_copy(tab8.at[r // 2], tabs, loc.at[3])
    to_scalars.start()
    to_scalars.wait()

    def all_landed(half):
        def one(k, carry):
            t = lax.rem(r + k, SEQ)
            arrival(land[half].at[t], a_r.at[t, half], (dp, t))
            return carry

        lax.fori_loop(1, SEQ, one, 0)

    lo = low_lanes((128, 128))
    zero = jnp.zeros((128, 128), BF)
    all_landed(0)

    def probabilities(s):
        qz = jnp.where(lo, zero, pltpu.roll(land_qk[s], 64, 1)) * jnp.asarray(0.125, BF)
        count = tabs[2, 64 + s]
        scores = [
            jnp.where(j < count, dot(land_qk[tabs[2, 4 * s + j]], qz, NT), -1e30) for j in range(4)
        ]
        top = jnp.max(
            jnp.maximum(jnp.maximum(scores[0], scores[1]), jnp.maximum(scores[2], scores[3])),
            axis=0,
            keepdims=True,
        )
        expo = [jnp.exp(v - top) for v in scores]
        total = jnp.sum((expo[0] + expo[1]) + (expo[2] + expo[3]), axis=0, keepdims=True)
        inv = 1.0 / total
        for j in range(4):
            probs[s, j] = expo[j] * inv

    def forward(g, carry):
        for n in range(4):
            probabilities(4 * g + n)
        return carry

    lax.fori_loop(0, 4, forward, 0)
    all_landed(1)

    def give_back(s, half):
        @pl.when(s != r)
        def _():
            push(back.at[s, half], home.at[r, half], b_s.at[s, half], b_r.at[r, half], (dp, s))

        @pl.when(s == r)
        def _():
            home[r, half] = back[s, half]

    def gradients(s):
        qk, vg = land_qk[s], land_vg[s]
        gz = jnp.where(lo, pltpu.roll(vg, 64, 1), zero)
        rhs = jnp.concatenate([jnp.where(lo, qk, zero), jnp.where(lo, zero, vg)], axis=0)
        slots = [tabs[2, 4 * s + j] for j in range(4)]
        keys = [land_qk[b] for b in slots]
        values = [land_vg[b] for b in slots]
        grad_p = [dot(v, gz, NT) for v in values]
        prob = [probs[s, j] for j in range(4)]
        prod = [a * g for a, g in zip(prob, grad_p)]
        delta = jnp.sum((prod[0] + prod[1]) + (prod[2] + prod[3]), axis=0, keepdims=True)
        low = [a.astype(BF) for a in prob]
        grad_s = [(a * (g - delta) * 0.125).astype(BF) for a, g in zip(prob, grad_p)]
        attn = dot(jnp.concatenate(values, axis=0), jnp.concatenate(low, axis=0), TN)
        grad_q = dot(jnp.concatenate(keys, axis=0), jnp.concatenate(grad_s, axis=0), TN)
        back[s, 0] = jnp.concatenate([attn[0:64], grad_q[64:128]], axis=0).T.astype(BF)
        for j in range(4):
            tiles[4 * s + j] = dot(jnp.concatenate([grad_s[j], low[j]], axis=1), rhs)

    def backward(g, carry):
        blocks = [lax.rem(r + 1 + 4 * g + n, SEQ) for n in range(4)]
        for s in blocks:
            gradients(s)
        for s in blocks:
            give_back(s, 0)
        return carry

    lax.fori_loop(0, 4, backward, 0)
    tiles[64] = jnp.zeros((128, 128), F32)

    def collect(n, carry):
        b = lax.rem(r + 1 + n, SEQ)
        total = tiles[tabs[b // 8, (b % 8) * 16]]
        for s in range(1, SEQ):
            total += tiles[tabs[b // 8, (b % 8) * 16 + s]]
        back[b, 1] = total.astype(BF)
        give_back(b, 1)
        return carry

    lax.fori_loop(0, SEQ, collect, 0)

    def came_home(t, half):
        @pl.when(t != r)
        def _():
            arrival(home.at[t, half], b_r.at[t, half], (dp, t))

    def half_rows(core):
        return pl.ds(pl.multiple_of(core * HALF, HALF), HALF)

    def take(core, half):
        for n in range(XS):
            i = core * XS + n
            came_home(2 * i, half)
            came_home(2 * i + 1, half)
            a, b = home[2 * i, half], home[2 * i + 1, half]
            rows = pl.ds(pl.multiple_of(i * ROWS, ROWS), ROWS)
            mix[rows, 256 * half : 256 * half + 128] = merge(a, b)
            mix[rows, 256 * half + 128 : 256 * half + 256] = merge_high(a, b)

    def product(core, n):
        if n == 0:
            return dot(mix[half_rows(core), 0:128], w_t[384:512, :])
        return dot(mix[half_rows(core), 128:512], w_t[0:384, :])

    def share(n):
        result = product(1 - c, n).astype(BF)
        for i in range(XS):
            part[n, i] = result[i * ROWS : i * ROWS + ROWS]
        sends.append(push(part.at[n, 0:XS], sib.at[n], sib_s.at[n], sib_r.at[n], sibling))

    def pass_on(n):
        result = product(c, n)
        arrival(sib.at[n], sib_r.at[n], sibling)
        for i in range(XS):
            total = result[i * ROWS : i * ROWS + ROWS] + sib[n, i].astype(F32)
            part[n, XS + i] = total.astype(BF)
        for k in NEAR:
            sends.append(
                push(
                    part.at[n, XS + turn(k)], far.at[n, x], far_s.at[n, k], far_r.at[n, x], at_x(k)
                )
            )

    def result_of(n, first):
        total = first.astype(F32) + part[n, XS + x].astype(F32)
        for k in NEAR:
            arrival(far.at[n, turn(k)], far_r.at[n, turn(k)], at_x(k))
            total += far[n, turn(k)].astype(F32)
        return total.astype(BF)

    def terms_out(n):
        if n == 0:
            cots = cot8[...].reshape(TEAM * ROWS, WIDTH)
            out_term = dot(mix[:, 0:128], cots, TN).astype(BF)
            for j in range(TEAM):
                block = out_term[:, 128 * j : 128 * j + 128]
                terms[0, 2 * j, :, 128:256] = block[0:64]
                terms[0, 2 * j + 1, :, 128:256] = block[64:128]
            in_term = dot(hid_t[...], mix[:, 128:256]).astype(BF)
            for s in range(SEQ):
                terms[0, s, :, 0:128] = in_term[64 * s : 64 * s + 64]
        else:
            in_term = dot(hid_t[...], mix[:, 256:512]).astype(BF)
            for s in range(SEQ):
                terms[1, s] = in_term[64 * s : 64 * s + 64]
        for h in range(4):
            for k in NEAR:
                sends.append(
                    push(
                        terms.at[n, 4 * h + lax.rem(y + k, YS)], from_y.at[n, y, h],
                        y_s.at[n, k, h], y_r.at[n, y, h], (dp, at_y(k)),
                    )
                )

    def along_z(n):
        for k in (1, 2, 3, 0):
            h = lax.rem(zh + k, 4)
            total = terms[n, 4 * h + y].astype(F32)
            for m in NEAR:
                t = lax.rem(y + m, YS)
                arrival(from_y.at[n, t, h], y_r.at[n, t, h], (dp, at_y(m)))
                total += from_y[n, t, h].astype(F32)
            to_z[n, h] = total.astype(BF)
            if k:
                sends.append(
                    push(
                        to_z.at[n, h], from_z.at[n, zh], z_s.at[n, h], z_r.at[n, zh],
                        (dp, h * YS + y),
                    )
                )

    def across(n):
        total = to_z[n, zh].astype(F32)
        for k in NEAR:
            h = lax.rem(zh + k, 4)
            arrival(from_z.at[n, h], z_r.at[n, h], (dp, at_z(k)))
            total += from_z[n, h].astype(F32)
        from_z[n, zh] = total.astype(BF)
        sends.append(push(from_z.at[n, zh], from_zl.at[n], zl_s.at[n], zl_r.at[n], partner))

    def to_team(n):
        arrival(from_zl.at[n], zl_r.at[n], partner)
        full[n, me] = (from_z[n, zh].astype(F32) + from_zl[n].astype(F32)).astype(BF)
        for k in range(1, TEAM):
            sends.append(
                push(
                    full.at[n, me], full.at[n, me], g_s.at[n, k], g_r.at[n, me], (team_peer(k), r)
                )
            )

    def from_team(n):
        for k in range(1, TEAM):
            i = lax.rem(p + k, TEAM)
            q = slot_of(i)
            arrival(full.at[n, q], g_r.at[n, q], (base + i, r))

    def out_piece(i):
        t = 2 * i + r % 2
        src = full.at[0, (i % 2) * XS + i // 2, :, 128:256]
        return t, remote(src, wob.at[r // 2], q_s.at[i], q_r.at[r // 2], (dp, t))

    for core in (1 - c, c):
        take(core, 0)
        if core is not c:
            share(0)
    terms_out(0)
    pass_on(0)
    along_z(0)
    take(1 - c, 1)
    take(c, 1)
    terms_out(1)
    share(1)
    across(0)
    pass_on(1)
    to_team(0)
    along_z(1)
    layer_out[...] = result_of(0, hid8[me])
    from_team(0)
    for i in range(TEAM):
        t, copy = out_piece(i)

        @pl.when(t != r)
        def _():
            copy.start()

        @pl.when(t == r)
        def _():
            wob[r // 2] = full[0, (i % 2) * XS + i // 2, :, 128:256]

    across(1)
    for i in range(TEAM):
        q = (i % 2) * XS + i // 2
        proj_grad[:, 0, 128 * i : 128 * i + 128] = full[0, q, :, 0:128].astype(F32)
    to_team(1)
    for j in range(TEAM):
        t, copy = out_piece(j)

        @pl.when(t != r)
        def _():
            arrival(wob.at[j], q_r.at[j], (dp, t))
            copy.wait_send()

        proj_grad[:, 3, 128 * j : 128 * j + 128] = wob[j].astype(F32)
    features_grad[...] = result_of(1, cot8[me])
    from_team(1)
    for i in range(TEAM):
        q = (i % 2) * XS + i // 2
        proj_grad[:, 1, 128 * i : 128 * i + 128] = full[1, q, :, 0:128].astype(F32)
        proj_grad[:, 2, 128 * i : 128 * i + 128] = full[1, q, :, 128:256].astype(F32)

    for copy in sends:
        copy.wait_send()

    @pl.when(spread)
    def _():
        for j in range(TEAM):
            t = 2 * j + r % 2

            @pl.when(t != r)
            def _():
                remote(
                    wt.at[j, :, 384:512], out_part(t), sc_s.at[j], sc_r, (dp, t)
                ).wait_send()

    def sent(k, carry):
        t = lax.rem(r + k, SEQ)
        for half in (0, 1):
            remote(
                stage.at[t, half], land[half].at[r], a_s.at[t, half], a_r.at[r, half], (dp, t)
            ).wait_send()
            remote(
                back.at[t, half], home.at[r, half], b_s.at[t, half], b_r.at[r, half], (dp, t)
            ).wait_send()
        return carry

    lax.fori_loop(1, SEQ, sent, 0)


def layer(hid, cot, wt, tab):
    vmem = pl.BlockSpec(memory_space=pltpu.VMEM)
    dma = pltpu.SemaphoreType.DMA
    tile = (128, 128)
    act = (ROWS, WIDTH)
    return pl.pallas_call(
        kernel,
        out_shape=[
            jax.ShapeDtypeStruct(act, BF),
            jax.ShapeDtypeStruct(act, BF),
            jax.ShapeDtypeStruct((SHARD, 4, WIDTH), F32),
        ],
        in_specs=[vmem] * 4,
        out_specs=[vmem] * 3,
        scratch_shapes=[
            pltpu.VMEM((TEAM, *act), BF),
            pltpu.VMEM((TEAM, *act), BF),
            pltpu.VMEM((WIDTH, TEAM * ROWS), BF),
            pltpu.VMEM((WIDTH, 512), BF),
            pltpu.VMEM((WIDTH, 128), BF),
            pltpu.VMEM((512, WIDTH), BF),
            pltpu.VMEM((TEAM, 8, 128), jnp.int32),
            pltpu.SMEM((8, 128), jnp.int32),
            pltpu.VMEM((SEQ, 2, *tile), BF),
            pltpu.VMEM((SEQ, *tile), BF),
            pltpu.VMEM((SEQ, *tile), BF),
            pltpu.VMEM((SEQ, 4, *tile), F32),
            pltpu.VMEM((SEQ * 4 + 1, *tile), F32),
            pltpu.VMEM((SEQ, 2, *tile), BF),
            pltpu.VMEM((SEQ, 2, *tile), BF),
            pltpu.VMEM((TEAM * ROWS, 512), BF),
            pltpu.VMEM((2, 2 * XS, *act), BF),
            pltpu.VMEM((2, XS, *act), BF),
            pltpu.VMEM((2, XS, *act), BF),
            pltpu.VMEM((2, SEQ, SHARD, 256), BF),
            pltpu.VMEM((2, YS, 4, SHARD, 256), BF),
            pltpu.VMEM((2, 4, SHARD, 256), BF),
            pltpu.VMEM((2, 4, SHARD, 256), BF),
            pltpu.VMEM((2, SHARD, 256), BF),
            pltpu.VMEM((2, TEAM, SHARD, 256), BF),
            pltpu.VMEM((TEAM, SHARD, 128), BF),
            dma((8,)), dma((8,)), dma((8,)), dma((8,)), dma((8,)), dma((8,)),
            dma((17,)), dma((16,)), dma((17,)), dma((16,)), dma((17,)), dma((16,)), dma((8,)), dma(()),
            dma((16, 2)), dma((16, 2)), dma((16, 2)), dma((16, 2)),
            dma((2,)), dma((2,)), dma((2, 4)), dma((2, 4)), dma((2, 4, 4)), dma((2, 4, 4)),
            dma((2, 4)), dma((2, 4)), dma((2,)), dma((2,)), dma((2, 8)), dma((2, 8)),
            dma((8,)), dma((8,)), dma((4,)),
        ],
        compiler_params=pltpu.CompilerParams(
            collective_id=1, has_side_effects=True, vmem_limit_bytes=VMEM_BYTES
        ),
    )(hid, cot, wt, tab)


def tables(order, neigh, count):
    spots = lax.iota(jnp.int32, SEQ)
    listing = 4 * spots[:, None] + lax.iota(jnp.int32, 4)[None, :]
    named = neigh[None] == order[:, None, None]
    users = jnp.min(jnp.where(named, listing[None], 64), axis=2)
    slots = jnp.sum(jnp.where(named, spots[:, None, None], 0), axis=0)
    flat = jnp.concatenate([users.reshape(-1), slots.reshape(-1), count, jnp.zeros((48,), jnp.int32)])
    return jnp.concatenate([flat.reshape(3, 128), jnp.zeros((5, 128), jnp.int32)])


def per_device(
    features, labels, label_table, proj_weight, block_order, neighbours, counts, cotangent
):
    onehot = (labels[0][:, None] == lax.iota(jnp.int32, label_table.shape[0])[None, :]).astype(BF)
    hidden = (
        features[0].astype(F32) + jnp.dot(onehot, label_table, preferred_element_type=F32)
    ).astype(BF)
    wt = proj_weight.reshape(SHARD, 4, TEAM, 128).transpose(2, 0, 1, 3).reshape(TEAM, SHARD, 512)
    tab = tables(block_order[0], neighbours[0], counts[0])
    layer_out, features_grad, proj_grad = layer(hidden, cotangent[0], wt, tab)
    return (layer_out[None], features_grad[None], proj_grad)


def solution(mesh):
    placed = (
        P("dp", "seq", None),
        P("dp", "seq"),
        P(),
        P("seq", None, None),
        P("dp", None),
        P("dp", None, None),
        P("dp", None),
        P("dp", "seq", None),
    )
    return jax.shard_map(
        per_device,
        mesh=mesh,
        in_specs=placed,
        out_specs=(P("dp", "seq", None), P("dp", "seq", None), P("seq", None, None)),
        check_vma=False,
    )
```

```python
import jax
import jax.numpy as jnp
from jax import lax
from jax.experimental import pallas as pl
from jax.experimental.pallas import tpu as pltpu
from jax.sharding import PartitionSpec as P

XS, YS, TEAM, SEQ, ROWS, WIDTH = 4, 4, 8, 16, 128, 1024
SHARD = WIDTH // SEQ
HALF = 4 * ROWS
BF, F32 = jnp.bfloat16, jnp.float32
NN = (((1,), (0,)), ((), ()))
NT = (((1,), (1,)), ((), ()))
TN = (((0,), (0,)), ((), ()))
VMEM_BYTES = 40 << 20
MESH = pl.DeviceIdType.MESH
NEAR = (1, 3, 2)


def dot(a, b, dims=NN):
    return lax.dot_general(a, b, dims, preferred_element_type=F32)


def remote(src, dst, send, recv, where):
    return pltpu.make_async_remote_copy(
        src_ref=src, dst_ref=dst, send_sem=send, recv_sem=recv, device_id=where, device_id_type=MESH
    )


def push(src, dst, send, recv, where):
    copy = remote(src, dst, send, recv, where)
    copy.start()
    return copy


def arrival(dst, recv, where):
    remote(dst, dst, recv, recv, where).wait_recv()


def low_lanes(shape):
    return lax.broadcasted_iota(jnp.int32, shape, 1) < 64


def merge(a, b):
    return jnp.where(low_lanes(a.shape), a, pltpu.roll(b, 64, 1))


def merge_high(a, b):
    return jnp.where(low_lanes(a.shape), pltpu.roll(a, 64, 1), b)


def kernel(
    hid, cot, wt, tab,
    layer_out, features_grad, proj_grad,
    hid8, cot8, hid_t, wg, wo, w_t, tab8, tabs, stage_qk, stage_v, stage_g, land_qk, land_v, land_g,
    v_full, probs, lows, tiles, back_a, back_q, back_kv, home_a, home_q, home_kv, mix,
    part, total, sib, far, terms, from_y, to_z, from_z, from_zl, full, wob,
    hid_s, hid_r, hid_h, cot_s, cot_r, cot_h, tab_s, tab_r, w_s, w_r, v_s, v_r, o_s, o_r, sc_s, sc_r,
    m_s, m_r, sib_s, sib_r, far_s, far_r, y_s, y_r, z_s, z_r, zl_s, zl_r, g_s, g_r, q_s, q_r, loc,
):
    dp, r = lax.axis_index("dp"), lax.axis_index("seq")
    zl, p = dp // TEAM, dp % TEAM
    x, c = p // 2, p % 2
    zh, y = r // YS, r % YS
    base = zl * TEAM
    me = c * XS + x
    sibling = (base + x * 2 + 1 - c, r)
    partner = (lax.rem(dp + TEAM, 2 * TEAM), r)

    def turn(k):
        return lax.rem(x + k, XS)

    def slot(k):
        return c * XS + turn(k)

    def at_x(k):
        return (base + turn(k) * 2 + c, r)

    def at_z(k):
        return lax.rem(zh + k, 4) * YS + y

    def at_y(k):
        return zh * YS + lax.rem(y + k, YS)

    def team_peer(k):
        return base + lax.rem(p + k, TEAM)

    def slot_of(q):
        return lax.rem(q, 2) * XS + q // 2

    barrier = pltpu.get_barrier_semaphore()
    greeted = [(team_peer(k), r) for k in range(1, TEAM)]
    greeted += [(dp, lax.rem(r + k, SEQ)) for k in range(1, SEQ)] + [partner]
    for where in greeted:
        pl.semaphore_signal(barrier, inc=1, device_id=where, device_id_type=MESH)
    pl.semaphore_wait(barrier, len(greeted))
    sends = []

    sources = (stage_qk, stage_v, stage_g, back_a, back_q, back_kv)
    targets = (land_qk, land_v, land_g, home_a, home_q, home_kv)

    def message(kind, t):
        return remote(
            sources[kind].at[t], targets[kind].at[r], m_s.at[kind, t], m_r.at[kind, r], (dp, t)
        )

    def give(kind, t):
        @pl.when(t != r)
        def _():
            message(kind, t).start()

        @pl.when(t == r)
        def _():
            targets[kind][r] = sources[kind][t]

    def got(kind, t):
        @pl.when(t != r)
        def _():
            arrival(targets[kind].at[t], m_r.at[kind, t], (dp, t))

    def got_all(kind):
        def one(k, carry):
            t = lax.rem(r + k, SEQ)
            arrival(targets[kind].at[t], m_r.at[kind, t], (dp, t))
            return carry

        lax.fori_loop(1, SEQ, one, 0)

    halves = (pl.ds(0, 64), pl.ds(64, 64))

    def spread_x(array, own, send, recv):
        for k in (1, 3):
            sends.append(push(own, array.at[me], send.at[k], recv.at[me], at_x(k)))
        sends.append(push(own, array.at[me], send.at[0], recv.at[me], sibling))

    def forward_x(array, send, recv, opposite):
        for k in (1, 3):
            q = slot(k)
            arrival(array.at[q], recv.at[q], at_x(k))
            h = k // 3
            piece = array.at[q, halves[h]]
            sends.append(push(piece, piece, send.at[4 + k], opposite.at[h], at_x(4 - k)))
            sends.append(push(array.at[q], array.at[q], send.at[1 + k], recv.at[q], sibling))

    def finish_x(array, send, recv, opposite):
        q = slot(2)
        for h, k in ((0, 1), (1, 3)):
            arrival(array.at[q, halves[h]], opposite.at[h], at_x(k))
        sends.append(push(array.at[q], array.at[q], send.at[6], recv.at[q], sibling))

    def other_core(array, recv):
        for k in range(XS):
            q = (1 - c) * XS + turn(k)
            arrival(array.at[q], recv.at[q], sibling)

    def rows_of(s):
        return pl.ds(pl.multiple_of(s * SHARD, SHARD), SHARD)

    def qk_part(s):
        return wg.at[rows_of(s), 0:256]

    def v_part(s):
        return wg.at[rows_of(s), 256:384]

    def out_part(s):
        return wg.at[rows_of(s), 384:512]

    own_w = pltpu.make_async_copy(wt.at[p, :, 0:384], wg.at[rows_of(r), 0:384], loc.at[0])
    own_w.start()
    mine_qk, mine_v = wt.at[p, :, 0:256], wt.at[p, :, 256:384]
    for k in NEAR:
        sends.append(push(mine_qk, qk_part(r), w_s.at[k], w_r.at[r], (dp, at_z(k))))
        sends.append(push(mine_v, v_part(r), v_s.at[k], v_r.at[r], (dp, at_y(k))))
    for k in NEAR:
        sends.append(push(mine_qk, qk_part(r), w_s.at[3 + k], w_r.at[r], (dp, at_y(k))))
        sends.append(push(mine_v, v_part(r), v_s.at[3 + k], v_r.at[r], (dp, at_z(k))))

    spread = r // 2 == p

    @pl.when(spread)
    def _():
        for j in range(TEAM):
            t = 2 * j + r % 2

            @pl.when(t != r)
            def _():
                push(wt.at[j, :, 384:512], out_part(t), sc_s.at[j], sc_r, (dp, t))

    keep_hid = pltpu.make_async_copy(hid, hid8.at[me], loc.at[1])
    keep_hid.start()
    keep_cot = pltpu.make_async_copy(cot, cot8.at[me], loc.at[2])
    keep_cot.start()
    spread_x(hid8, hid, hid_s, hid_r)
    for k in range(1, TEAM):
        sends.append(push(tab, tab8.at[me], tab_s.at[k], tab_r.at[me], (team_peer(k), r)))

    for n, k in enumerate(NEAR):
        s = at_z(k)
        arrival(qk_part(s), w_r.at[s], (dp, s))
        for m in NEAR:
            sends.append(
                push(qk_part(s), qk_part(s), w_s.at[7 + n * 3 + m], w_r.at[s], (dp, at_y(m)))
            )
        s = at_y(k)
        arrival(v_part(s), v_r.at[s], (dp, s))
        for m in NEAR:
            sends.append(
                push(v_part(s), v_part(s), v_s.at[7 + n * 3 + m], v_r.at[s], (dp, at_z(m)))
            )

    forward_x(hid8, hid_s, hid_r, hid_h)
    spread_x(cot8, cot, cot_s, cot_r)

    piece = out_part(r)

    @pl.when(spread)
    def _():
        copy = pltpu.make_async_copy(wt.at[p, :, 384:512], piece, loc.at[3])
        copy.start()
        copy.wait()

    @pl.when(jnp.logical_not(spread))
    def _():
        arrival(piece, sc_r, (dp, r))

    for k in NEAR:
        sends.append(push(piece, piece, o_s.at[k], o_r.at[r], (dp, at_z(k))))
    for k in NEAR:
        sends.append(push(piece, piece, o_s.at[3 + k], o_r.at[r], (dp, at_y(k))))
    finish_x(hid8, hid_s, hid_r, hid_h)
    for n, k in enumerate(NEAR):
        s = at_z(k)
        arrival(out_part(s), o_r.at[s], (dp, s))
        for m in NEAR:
            sends.append(
                push(out_part(s), out_part(s), o_s.at[7 + n * 3 + m], o_r.at[s], (dp, at_y(m)))
            )

    def from_all_y(piece_of, sems):
        for m in NEAR:
            for k in range(4):
                s = lax.rem(zh + k, 4) * YS + lax.rem(y + m, YS)
                arrival(piece_of(s), sems.at[s], (dp, s))

    def group_rows(array, core):
        block = array[pl.ds(pl.multiple_of(core * XS, XS), XS)]
        return block.reshape(HALF, array.shape[2])

    def packed(stage, kind, core, result):
        for n in range(XS):
            top = result[n * ROWS : n * ROWS + 64]
            bottom = result[n * ROWS + 64 : n * ROWS + ROWS]
            i = core * XS + n
            stage[2 * i] = merge(top, bottom)
            stage[2 * i + 1] = merge_high(top, bottom)
            give(kind, 2 * i)
            give(kind, 2 * i + 1)

    from_all_y(qk_part, w_r)
    own_w.wait()
    keep_hid.wait()
    for core in (c, 1 - c):
        if core is not c:
            other_core(hid8, hid_r)
        queries_keys = dot(group_rows(hid8, core), wg[:, 0:256]).astype(BF)
        for n in range(XS):
            rows = queries_keys[n * ROWS : n * ROWS + ROWS]
            q, k = rows[:, 0:128], rows[:, 128:256]
            i = core * XS + n
            stage_qk[2 * i] = merge(q, k)
            stage_qk[2 * i + 1] = merge_high(q, k)
            give(0, 2 * i)
            give(0, 2 * i + 1)

    forward_x(cot8, cot_s, cot_r, cot_h)
    for m in NEAR:
        for k in range(1, 4):
            s = lax.rem(zh + k, 4) * YS + lax.rem(y + m, YS)
            arrival(v_part(s), v_r.at[s], (dp, s))
    for k in NEAR:
        s = at_z(k)
        arrival(v_part(s), v_r.at[s], (dp, s))
    for core in (c, 1 - c):
        packed(stage_v, 1, core, dot(group_rows(hid8, core), wg[:, 256:384]).astype(BF))
    from_all_y(out_part, o_r)
    for j in range(TEAM):
        block = wg[128 * j : 128 * j + 128, 384:512]
        wo[128 * j : 128 * j + 128, :] = block.T
        w_t[384:512, 128 * j : 128 * j + 128] = block
    finish_x(cot8, cot_s, cot_r, cot_h)
    keep_cot.wait()
    for core in (c, 1 - c):
        if core is not c:
            other_core(cot8, cot_r)
        packed(stage_g, 2, core, dot(group_rows(cot8, core), wo[...]).astype(BF))

    for n in range(3):
        w_t[128 * n : 128 * n + 128, :] = wg[:, 128 * n : 128 * n + 128].T
    for q in range(TEAM):
        hid_t[:, 128 * q : 128 * q + 128] = hid8[q].T

    for k in range(1, TEAM):
        i = lax.rem(p + k, TEAM)
        q = slot_of(i)
        arrival(tab8.at[q], tab_r.at[q], (base + i, r))
    tab8[me] = tab[...]
    to_scalars = pltpu.make_async_copy(tab8.at[r // 2], tabs, loc.at[3])
    to_scalars.start()
    to_scalars.wait()

    lo = low_lanes((128, 128))
    zero = jnp.zeros((128, 128), BF)
    got_all(0)

    def probabilities(s):
        qz = jnp.where(lo, zero, pltpu.roll(land_qk[s], 64, 1)) * jnp.asarray(0.125, BF)
        count = tabs[2, 64 + s]
        scores = [
            jnp.where(j < count, dot(land_qk[tabs[2, 4 * s + j]], qz, NT), -1e30) for j in range(4)
        ]
        top = jnp.max(
            jnp.maximum(jnp.maximum(scores[0], scores[1]), jnp.maximum(scores[2], scores[3])),
            axis=0,
            keepdims=True,
        )
        expo = [jnp.exp(v - top) for v in scores]
        total = jnp.sum((expo[0] + expo[1]) + (expo[2] + expo[3]), axis=0, keepdims=True)
        inv = 1.0 / total
        for j in range(4):
            prob = expo[j] * inv
            probs[s, j] = prob
            lows[s, 128 * j : 128 * j + 128] = prob.astype(BF)

    def forward(g, carry):
        for n in range(4):
            probabilities(4 * g + n)
        return carry

    lax.fori_loop(0, 4, forward, 0)
    got_all(1)
    for s in range(SEQ):
        v_full[s, 0:64] = land_v[s]
        v_full[s, 64:128] = pltpu.roll(land_v[s], 64, 1)

    def blocks_of(g):
        return [lax.rem(r + 1 + 4 * g + n, SEQ) for n in range(4)]

    def attention(g, carry):
        for s in blocks_of(g):
            values = [v_full[tabs[2, 4 * s + j]] for j in range(4)]
            attn = dot(jnp.concatenate(values, axis=0), lows[s], TN).T.astype(BF)
            back_a[s] = merge(attn[0:64], attn[64:128])
        for s in blocks_of(g):
            give(3, s)
        return carry

    lax.fori_loop(0, 4, attention, 0)
    got_all(2)

    def gradients(s):
        qk, grad = land_qk[s], land_g[s]
        turned = pltpu.roll(grad, 64, 1)
        gz = jnp.where(lo, jnp.concatenate([grad, turned], axis=0), zero)
        gv = jnp.where(lo, zero, jnp.concatenate([turned, grad], axis=0))
        rhs = jnp.concatenate([jnp.where(lo, qk, zero), gv], axis=0)
        slots = [tabs[2, 4 * s + j] for j in range(4)]
        keys = [land_qk[b] for b in slots]
        grad_p = [dot(v_full[b], gz, NT) for b in slots]
        prob = [probs[s, j] for j in range(4)]
        prod = [a * g for a, g in zip(prob, grad_p)]
        delta = jnp.sum((prod[0] + prod[1]) + (prod[2] + prod[3]), axis=0, keepdims=True)
        grad_s = [(a * (g - delta) * 0.125).astype(BF) for a, g in zip(prob, grad_p)]
        grad_q = dot(
            jnp.concatenate(keys, axis=0), jnp.concatenate(grad_s, axis=0), TN
        ).T.astype(BF)
        back_q[s] = merge_high(grad_q[0:64], grad_q[64:128])
        for j in range(4):
            low = lows[s, 128 * j : 128 * j + 128]
            tiles[4 * s + j] = dot(jnp.concatenate([grad_s[j], low], axis=1), rhs)

    def backward(g, carry):
        for s in blocks_of(g):
            gradients(s)
        for s in blocks_of(g):
            give(4, s)
        return carry

    lax.fori_loop(0, 4, backward, 0)
    tiles[64] = jnp.zeros((128, 128), F32)

    def collect(n, carry):
        b = lax.rem(r + 1 + n, SEQ)
        total = tiles[tabs[b // 8, (b % 8) * 16]]
        for s in range(1, SEQ):
            total += tiles[tabs[b // 8, (b % 8) * 16 + s]]
        back_kv[b] = total.astype(BF)
        give(5, b)
        return carry

    lax.fori_loop(0, SEQ, collect, 0)

    def half_rows(core):
        return pl.ds(pl.multiple_of(core * HALF, HALF), HALF)

    def take(core, kind):
        for n in range(XS):
            i = core * XS + n
            got(kind, 2 * i)
            got(kind, 2 * i + 1)
            a, b = targets[kind][2 * i], targets[kind][2 * i + 1]
            start = pl.multiple_of(i * ROWS, ROWS)
            if kind == 5:
                mix[pl.ds(start, ROWS), 256:384] = merge(a, b)
                mix[pl.ds(start, ROWS), 384:512] = merge_high(a, b)
            else:
                cols = pl.ds(128 * (kind - 3), 128)
                mix[pl.ds(start, 64), cols] = merge(a, b)
                mix[pl.ds(start + 64, 64), cols] = merge_high(a, b)

    def product(core, n):
        if n == 0:
            return dot(mix[half_rows(core), 0:128], w_t[384:512, :])
        return dot(mix[half_rows(core), 128:512], w_t[0:384, :])

    def share(n):
        result = product(1 - c, n).astype(BF)
        for i in range(XS):
            part[n, i] = result[i * ROWS : i * ROWS + ROWS]
        for k in (1, 3, 2, 0):
            i = turn(k)
            sends.append(push(part.at[n, i], sib.at[n, i], sib_s.at[n, k], sib_r.at[n, i], sibling))

    def pass_on(n):
        result = product(c, n)
        for i in range(XS):
            total[i] = result[i * ROWS : i * ROWS + ROWS]
        for k in (1, 3, 2, 0):
            i = turn(k)
            arrival(sib.at[n, i], sib_r.at[n, i], sibling)
            part[n, XS + i] = (total[i] + sib[n, i].astype(F32)).astype(BF)
            if k:
                sends.append(
                    push(part.at[n, XS + i], far.at[n, x], far_s.at[n, k], far_r.at[n, x], at_x(k))
                )

    def result_of(n, first):
        result = first.astype(F32) + part[n, XS + x].astype(F32)
        for k in NEAR:
            arrival(far.at[n, turn(k)], far_r.at[n, turn(k)], at_x(k))
            result += far[n, turn(k)].astype(F32)
        return result.astype(BF)

    def terms_out(n):
        if n == 0:
            cots = cot8[...].reshape(TEAM * ROWS, WIDTH)
            out_term = dot(mix[:, 0:128], cots, TN).astype(BF)
            for j in range(TEAM):
                block = out_term[:, 128 * j : 128 * j + 128]
                terms[0, 2 * j, :, 128:256] = block[0:64]
                terms[0, 2 * j + 1, :, 128:256] = block[64:128]
            in_term = dot(hid_t[...], mix[:, 128:256]).astype(BF)
            for s in range(SEQ):
                terms[0, s, :, 0:128] = in_term[64 * s : 64 * s + 64]
        for h in range(4):
            if n == 1:
                in_term = dot(hid_t[256 * h : 256 * h + 256], mix[:, 256:512]).astype(BF)
                for m in range(YS):
                    terms[1, 4 * h + m] = in_term[64 * m : 64 * m + 64]
            for k in NEAR:
                sends.append(
                    push(
                        terms.at[n, 4 * h + lax.rem(y + k, YS)], from_y.at[n, y, h],
                        y_s.at[n, k, h], y_r.at[n, y, h], (dp, at_y(k)),
                    )
                )

    def along_z(n):
        for k in (1, 2, 3, 0):
            h = lax.rem(zh + k, 4)
            total = terms[n, 4 * h + y].astype(F32)
            for m in NEAR:
                t = lax.rem(y + m, YS)
                arrival(from_y.at[n, t, h], y_r.at[n, t, h], (dp, at_y(m)))
                total += from_y[n, t, h].astype(F32)
            to_z[n, h] = total.astype(BF)
            if k:
                sends.append(
                    push(
                        to_z.at[n, h], from_z.at[n, zh], z_s.at[n, h], z_r.at[n, zh],
                        (dp, h * YS + y),
                    )
                )

    def across(n):
        total = to_z[n, zh].astype(F32)
        for k in NEAR:
            h = lax.rem(zh + k, 4)
            arrival(from_z.at[n, h], z_r.at[n, h], (dp, at_z(k)))
            total += from_z[n, h].astype(F32)
        from_z[n, zh] = total.astype(BF)
        sends.append(push(from_z.at[n, zh], from_zl.at[n], zl_s.at[n], zl_r.at[n], partner))

    def to_team(n):
        arrival(from_zl.at[n], zl_r.at[n], partner)
        full[n, me] = (from_z[n, zh].astype(F32) + from_zl[n].astype(F32)).astype(BF)
        for k in range(1, TEAM):
            sends.append(
                push(
                    full.at[n, me], full.at[n, me], g_s.at[n, k], g_r.at[n, me], (team_peer(k), r)
                )
            )

    def from_team(n):
        for k in range(1, TEAM):
            i = lax.rem(p + k, TEAM)
            q = slot_of(i)
            arrival(full.at[n, q], g_r.at[n, q], (base + i, r))

    def out_piece(i):
        t = 2 * i + r % 2
        src = full.at[0, (i % 2) * XS + i // 2, :, 128:256]
        return t, remote(src, wob.at[r // 2], q_s.at[i], q_r.at[r // 2], (dp, t))

    take(1 - c, 3)
    share(0)
    take(c, 3)
    pass_on(0)
    take(1 - c, 4)
    take(c, 4)
    terms_out(0)
    take(1 - c, 5)
    take(c, 5)
    terms_out(1)
    share(1)
    along_z(0)
    pass_on(1)
    across(0)
    to_team(0)
    along_z(1)
    layer_out[...] = result_of(0, hid8[me])
    from_team(0)
    for i in range(TEAM):
        t, copy = out_piece(i)

        @pl.when(t != r)
        def _():
            copy.start()

        @pl.when(t == r)
        def _():
            wob[r // 2] = full[0, (i % 2) * XS + i // 2, :, 128:256]

    across(1)
    for i in range(TEAM):
        q = (i % 2) * XS + i // 2
        proj_grad[:, 0, 128 * i : 128 * i + 128] = full[0, q, :, 0:128].astype(F32)
    to_team(1)
    for j in range(TEAM):
        t, copy = out_piece(j)

        @pl.when(t != r)
        def _():
            arrival(wob.at[j], q_r.at[j], (dp, t))
            copy.wait_send()

        proj_grad[:, 3, 128 * j : 128 * j + 128] = wob[j].astype(F32)
    features_grad[...] = result_of(1, cot8[me])
    from_team(1)
    for i in range(TEAM):
        q = (i % 2) * XS + i // 2
        proj_grad[:, 1, 128 * i : 128 * i + 128] = full[1, q, :, 0:128].astype(F32)
        proj_grad[:, 2, 128 * i : 128 * i + 128] = full[1, q, :, 128:256].astype(F32)

    for copy in sends:
        copy.wait_send()

    @pl.when(spread)
    def _():
        for j in range(TEAM):
            t = 2 * j + r % 2

            @pl.when(t != r)
            def _():
                remote(
                    wt.at[j, :, 384:512], out_part(t), sc_s.at[j], sc_r, (dp, t)
                ).wait_send()

    def sent(k, carry):
        t = lax.rem(r + k, SEQ)
        for kind in range(6):
            message(kind, t).wait_send()
        return carry

    lax.fori_loop(1, SEQ, sent, 0)


def layer(hid, cot, wt, tab):
    vmem = pl.BlockSpec(memory_space=pltpu.VMEM)
    dma = pltpu.SemaphoreType.DMA
    tile, small = (128, 128), (64, 128)
    act = (ROWS, WIDTH)
    return pl.pallas_call(
        kernel,
        out_shape=[
            jax.ShapeDtypeStruct(act, BF),
            jax.ShapeDtypeStruct(act, BF),
            jax.ShapeDtypeStruct((SHARD, 4, WIDTH), F32),
        ],
        in_specs=[vmem] * 4,
        out_specs=[vmem] * 3,
        scratch_shapes=[
            pltpu.VMEM((TEAM, *act), BF),
            pltpu.VMEM((TEAM, *act), BF),
            pltpu.VMEM((WIDTH, TEAM * ROWS), BF),
            pltpu.VMEM((WIDTH, 512), BF),
            pltpu.VMEM((WIDTH, 128), BF),
            pltpu.VMEM((512, WIDTH), BF),
            pltpu.VMEM((TEAM, 8, 128), jnp.int32),
            pltpu.SMEM((8, 128), jnp.int32),
            pltpu.VMEM((SEQ, *tile), BF),
            pltpu.VMEM((SEQ, *small), BF),
            pltpu.VMEM((SEQ, *small), BF),
            pltpu.VMEM((SEQ, *tile), BF),
            pltpu.VMEM((SEQ, *small), BF),
            pltpu.VMEM((SEQ, *small), BF),
            pltpu.VMEM((SEQ, *tile), BF),
            pltpu.VMEM((SEQ, 4, *tile), F32),
            pltpu.VMEM((SEQ, 512, 128), BF),
            pltpu.VMEM((SEQ * 4 + 1, *tile), F32),
            pltpu.VMEM((SEQ, *small), BF),
            pltpu.VMEM((SEQ, *small), BF),
            pltpu.VMEM((SEQ, *tile), BF),
            pltpu.VMEM((SEQ, *small), BF),
            pltpu.VMEM((SEQ, *small), BF),
            pltpu.VMEM((SEQ, *tile), BF),
            pltpu.VMEM((TEAM * ROWS, 512), BF),
            pltpu.VMEM((2, 2 * XS, *act), BF),
            pltpu.VMEM((XS, *act), F32),
            pltpu.VMEM((2, XS, *act), BF),
            pltpu.VMEM((2, XS, *act), BF),
            pltpu.VMEM((2, SEQ, SHARD, 256), BF),
            pltpu.VMEM((2, YS, 4, SHARD, 256), BF),
            pltpu.VMEM((2, 4, SHARD, 256), BF),
            pltpu.VMEM((2, 4, SHARD, 256), BF),
            pltpu.VMEM((2, SHARD, 256), BF),
            pltpu.VMEM((2, TEAM, SHARD, 256), BF),
            pltpu.VMEM((TEAM, SHARD, 128), BF),
            dma((8,)), dma((8,)), dma((2,)), dma((8,)), dma((8,)), dma((2,)), dma((8,)), dma((8,)),
            dma((17,)), dma((16,)), dma((17,)), dma((16,)), dma((17,)), dma((16,)), dma((8,)), dma(()),
            dma((6, 16)), dma((6, 16)),
            dma((2, 4)), dma((2, 4)), dma((2, 4)), dma((2, 4)), dma((2, 4, 4)), dma((2, 4, 4)),
            dma((2, 4)), dma((2, 4)), dma((2,)), dma((2,)), dma((2, 8)), dma((2, 8)),
            dma((8,)), dma((8,)), dma((4,)),
        ],
        compiler_params=pltpu.CompilerParams(
            collective_id=1, has_side_effects=True, vmem_limit_bytes=VMEM_BYTES
        ),
    )(hid, cot, wt, tab)


def tables(order, neigh, count):
    spots = lax.iota(jnp.int32, SEQ)
    listing = 4 * spots[:, None] + lax.iota(jnp.int32, 4)[None, :]
    named = neigh[None] == order[:, None, None]
    users = jnp.min(jnp.where(named, listing[None], 64), axis=2)
    slots = jnp.sum(jnp.where(named, spots[:, None, None], 0), axis=0)
    flat = jnp.concatenate([users.reshape(-1), slots.reshape(-1), count, jnp.zeros((48,), jnp.int32)])
    return jnp.concatenate([flat.reshape(3, 128), jnp.zeros((5, 128), jnp.int32)])


def per_device(
    features, labels, label_table, proj_weight, block_order, neighbours, counts, cotangent
):
    onehot = (labels[0][:, None] == lax.iota(jnp.int32, label_table.shape[0])[None, :]).astype(BF)
    hidden = (
        features[0].astype(F32) + jnp.dot(onehot, label_table, preferred_element_type=F32)
    ).astype(BF)
    wt = proj_weight.reshape(SHARD, 4, TEAM, 128).transpose(2, 0, 1, 3).reshape(TEAM, SHARD, 512)
    tab = tables(block_order[0], neighbours[0], counts[0])
    layer_out, features_grad, proj_grad = layer(hidden, cotangent[0], wt, tab)
    return (layer_out[None], features_grad[None], proj_grad)


def solution(mesh):
    placed = (
        P("dp", "seq", None),
        P("dp", "seq"),
        P(),
        P("seq", None, None),
        P("dp", None),
        P("dp", None, None),
        P("dp", None),
        P("dp", "seq", None),
    )
    return jax.shard_map(
        per_device,
        mesh=mesh,
        in_specs=placed,
        out_specs=(P("dp", "seq", None), P("dp", "seq", None), P("seq", None, None)),
        check_vma=False,
    )
```

```python
import jax
import jax.numpy as jnp
from jax import lax
from jax.experimental import pallas as pl
from jax.experimental.pallas import tpu as pltpu
from jax.sharding import PartitionSpec as P

XS, YS, TEAM, SEQ, ROWS, WIDTH = 4, 4, 8, 16, 128, 1024
SHARD = WIDTH // SEQ
HALF = 4 * ROWS
BF, F32 = jnp.bfloat16, jnp.float32
NN = (((1,), (0,)), ((), ()))
NT = (((1,), (1,)), ((), ()))
TN = (((0,), (0,)), ((), ()))
VMEM_BYTES = 40 << 20
MESH = pl.DeviceIdType.MESH
NEAR = (1, 3, 2)


def dot(a, b, dims=NN):
    return lax.dot_general(a, b, dims, preferred_element_type=F32)


def remote(src, dst, send, recv, where):
    return pltpu.make_async_remote_copy(
        src_ref=src, dst_ref=dst, send_sem=send, recv_sem=recv, device_id=where, device_id_type=MESH
    )


def push(src, dst, send, recv, where):
    copy = remote(src, dst, send, recv, where)
    copy.start()
    return copy


def arrival(dst, recv, where):
    remote(dst, dst, recv, recv, where).wait_recv()


def low_lanes(shape):
    return lax.broadcasted_iota(jnp.int32, shape, 1) < 64


def merge(a, b):
    return jnp.where(low_lanes(a.shape), a, pltpu.roll(b, 64, 1))


def merge_high(a, b):
    return jnp.where(low_lanes(a.shape), pltpu.roll(a, 64, 1), b)


def kernel(
    feat, labels, table, order, neigh, counts, cot, wt,
    layer_out, features_grad, proj_grad,
    hid, tab, hid8, cot8, hid_t, wg, wo, w_t, tab8, raw, slots_of, users_of, stage_qk, stage_v, stage_g, land_qk, land_v, land_g,
    v_full, probs, lows, tiles, back_a, back_q, back_k, back_v, home_a, home_q, home_k, home_v, mix,
    part, total, sib, far, terms_a, terms_k, terms_v, from_y_a, from_y_k, from_y_v,
    to_z_a, to_z_k, to_z_v, from_z_a, from_z_k, from_z_v, full_a, full_k, full_v, wob,
    hid_s, hid_r, hid_h, cot_s, cot_r, cot_h, tab_s, tab_r, w_s, w_r, v_s, v_r, o_s, o_r, sc_s, sc_r,
    m_s, m_r, sib_s, sib_r, far_s, far_r, y_s, y_r, z_s, z_r, g_s, g_r, q_s, q_r, loc,
):
    dp, r = lax.axis_index("dp"), lax.axis_index("seq")
    zl, p = dp // TEAM, dp % TEAM
    x, c = p // 2, p % 2
    zh, y = r // YS, r % YS
    base = zl * TEAM
    me = c * XS + x
    sibling = (base + x * 2 + 1 - c, r)
    across = lax.rem(dp + TEAM, 2 * TEAM)

    def turn(k):
        return lax.rem(x + k, XS)

    def slot(k):
        return c * XS + turn(k)

    def at_x(k):
        return (base + turn(k) * 2 + c, r)

    def at_z(k):
        return lax.rem(zh + k, 4) * YS + y

    def at_y(k):
        return zh * YS + lax.rem(y + k, YS)

    def team_peer(k):
        return base + lax.rem(p + k, TEAM)

    def slot_of(q):
        return lax.rem(q, 2) * XS + q // 2

    barrier = pltpu.get_barrier_semaphore()
    greeted = [(lax.rem(dp + k, 2 * TEAM), r) for k in range(1, 2 * TEAM)]
    greeted += [(dp, lax.rem(r + k, SEQ)) for k in range(1, SEQ)]
    greeted += [(across, at_z(k)) for k in (1, 2, 3)]
    for where in greeted:
        pl.semaphore_signal(barrier, inc=1, device_id=where, device_id_type=MESH)
    chosen = lax.broadcasted_iota(jnp.int32, (table.shape[0], ROWS), 0) == labels[...]
    embedded = dot(chosen.astype(F32).astype(BF), table[...], TN)
    hid[...] = (feat[...].astype(F32) + embedded).astype(BF)
    tab[...] = jnp.zeros_like(tab)
    tab[0:1, 0:SEQ] = order[...]
    tab[1:2, 0:SEQ] = counts[...]
    tab[2:6, 0:SEQ] = neigh[...]
    pl.semaphore_wait(barrier, len(greeted))
    sends = []

    sources = (stage_qk, stage_v, stage_g, back_a, back_q, back_k, back_v)
    targets = (land_qk, land_v, land_g, home_a, home_q, home_k, home_v)

    def message(kind, t):
        return remote(
            sources[kind].at[t], targets[kind].at[r], m_s.at[kind, t], m_r.at[kind, r], (dp, t)
        )

    def after(k):
        return lax.rem(r + k, SEQ)

    def before(k):
        return lax.rem(r + SEQ - k, SEQ)

    def keep(kind):
        targets[kind][r] = sources[kind][r]

    def arrived(kind, t):
        arrival(targets[kind].at[t], m_r.at[kind, t], (dp, t))

    def give_all(kind):
        def one(k, carry):
            message(kind, after(k)).start()
            return carry

        lax.fori_loop(1, SEQ, one, 0)
        keep(kind)

    def got_all(kind):
        def one(k, carry):
            arrived(kind, before(k))
            return carry

        lax.fori_loop(1, SEQ, one, 0)

    halves = (pl.ds(0, 64), pl.ds(64, 64))

    def spread_x(array, own, send, recv):
        for k in (1, 3):
            sends.append(push(own, array.at[me], send.at[k], recv.at[me], at_x(k)))
        sends.append(push(own, array.at[me], send.at[0], recv.at[me], sibling))

    def forward_x(array, send, recv, opposite):
        for k in (1, 3):
            q = slot(k)
            arrival(array.at[q], recv.at[q], at_x(k))
            h = k // 3
            piece = array.at[q, halves[h]]
            sends.append(push(piece, piece, send.at[4 + k], opposite.at[h], at_x(4 - k)))
            sends.append(push(array.at[q], array.at[q], send.at[1 + k], recv.at[q], sibling))

    def finish_x(array, send, recv, opposite):
        q = slot(2)
        for h, k in ((0, 1), (1, 3)):
            arrival(array.at[q, halves[h]], opposite.at[h], at_x(k))
        sends.append(push(array.at[q], array.at[q], send.at[6], recv.at[q], sibling))

    def other_core(array, recv):
        for k in range(XS):
            q = (1 - c) * XS + turn(k)
            arrival(array.at[q], recv.at[q], sibling)

    def rows_of(s):
        return pl.ds(pl.multiple_of(s * SHARD, SHARD), SHARD)

    def qk_part(s):
        return wg.at[rows_of(s), 0:256]

    def v_part(s):
        return wg.at[rows_of(s), 256:384]

    def out_part(s):
        return wg.at[rows_of(s), 384:512]

    own_w = pltpu.make_async_copy(wt.at[p, :, 0:384], wg.at[rows_of(r), 0:384], loc.at[0])
    own_w.start()
    mine_qk, mine_v = wt.at[p, :, 0:256], wt.at[p, :, 256:384]
    for k in NEAR:
        sends.append(push(mine_qk, qk_part(r), w_s.at[k], w_r.at[r], (dp, at_z(k))))
    for k in NEAR:
        sends.append(push(mine_qk, qk_part(r), w_s.at[3 + k], w_r.at[r], (dp, at_y(k))))
    for k in NEAR:
        sends.append(push(mine_v, v_part(r), v_s.at[k], v_r.at[r], (dp, at_z(k))))
    for k in NEAR:
        sends.append(push(mine_v, v_part(r), v_s.at[3 + k], v_r.at[r], (dp, at_y(k))))

    spread = r // 2 == p

    @pl.when(spread)
    def _():
        for j in range(TEAM):
            t = 2 * j + r % 2

            @pl.when(t != r)
            def _():
                push(wt.at[j, :, 384:512], out_part(t), sc_s.at[j], sc_r, (dp, t))

    keep_hid = pltpu.make_async_copy(hid, hid8.at[me], loc.at[1])
    keep_hid.start()
    keep_cot = pltpu.make_async_copy(cot, cot8.at[me], loc.at[2])
    keep_cot.start()
    spread_x(hid8, hid, hid_s, hid_r)
    for k in range(1, TEAM):
        sends.append(push(tab, tab8.at[me], tab_s.at[k], tab_r.at[me], (team_peer(k), r)))

    for n, k in enumerate(NEAR):
        s = at_z(k)
        arrival(qk_part(s), w_r.at[s], (dp, s))
        for m in NEAR:
            sends.append(
                push(qk_part(s), qk_part(s), w_s.at[7 + n * 3 + m], w_r.at[s], (dp, at_y(m)))
            )

    forward_x(hid8, hid_s, hid_r, hid_h)
    spread_x(cot8, cot, cot_s, cot_r)
    for n, k in enumerate(NEAR):
        s = at_z(k)
        arrival(v_part(s), v_r.at[s], (dp, s))
        for m in NEAR:
            sends.append(
                push(v_part(s), v_part(s), v_s.at[7 + n * 3 + m], v_r.at[s], (dp, at_y(m)))
            )

    piece = out_part(r)

    @pl.when(spread)
    def _():
        copy = pltpu.make_async_copy(wt.at[p, :, 384:512], piece, loc.at[3])
        copy.start()
        copy.wait()

    @pl.when(jnp.logical_not(spread))
    def _():
        arrival(piece, sc_r, (dp, r))

    for k in NEAR:
        sends.append(push(piece, piece, o_s.at[k], o_r.at[r], (dp, at_z(k))))
    for k in NEAR:
        sends.append(push(piece, piece, o_s.at[3 + k], o_r.at[r], (dp, at_y(k))))
    finish_x(hid8, hid_s, hid_r, hid_h)
    for n, k in enumerate(NEAR):
        s = at_z(k)
        arrival(out_part(s), o_r.at[s], (dp, s))
        for m in NEAR:
            sends.append(
                push(out_part(s), out_part(s), o_s.at[7 + n * 3 + m], o_r.at[s], (dp, at_y(m)))
            )

    def from_all_y(piece_of, sems):
        for m in NEAR:
            for k in range(4):
                s = lax.rem(zh + k, 4) * YS + lax.rem(y + m, YS)
                arrival(piece_of(s), sems.at[s], (dp, s))

    def group_rows(array, core):
        block = array[pl.ds(pl.multiple_of(core * XS, XS), XS)]
        return block.reshape(HALF, array.shape[2])

    def packed(stage, core, result):
        for n in range(XS):
            top = result[n * ROWS : n * ROWS + 64]
            bottom = result[n * ROWS + 64 : n * ROWS + ROWS]
            i = core * XS + n
            stage[2 * i] = merge(top, bottom)
            stage[2 * i + 1] = merge_high(top, bottom)

    from_all_y(qk_part, w_r)
    own_w.wait()
    keep_hid.wait()
    for core in (c, 1 - c):
        if core is not c:
            other_core(hid8, hid_r)
        queries_keys = dot(group_rows(hid8, core), wg[:, 0:256]).astype(BF)
        for n in range(XS):
            rows = queries_keys[n * ROWS : n * ROWS + ROWS]
            q, k = rows[:, 0:128], rows[:, 128:256]
            i = core * XS + n
            stage_qk[2 * i] = merge(q, k)
            stage_qk[2 * i + 1] = merge_high(q, k)
    give_all(0)

    forward_x(cot8, cot_s, cot_r, cot_h)
    from_all_y(v_part, v_r)
    for core in (c, 1 - c):
        packed(stage_v, core, dot(group_rows(hid8, core), wg[:, 256:384]).astype(BF))
    give_all(1)
    from_all_y(out_part, o_r)
    for j in range(TEAM):
        block = wg[128 * j : 128 * j + 128, 384:512]
        wo[128 * j : 128 * j + 128, :] = block.T
        w_t[384:512, 128 * j : 128 * j + 128] = block
    finish_x(cot8, cot_s, cot_r, cot_h)
    keep_cot.wait()
    for core in (c, 1 - c):
        if core is not c:
            other_core(cot8, cot_r)
        packed(stage_g, core, dot(group_rows(cot8, core), wo[...]).astype(BF))

    give_all(2)

    for n in range(3):
        w_t[128 * n : 128 * n + 128, :] = wg[:, 128 * n : 128 * n + 128].T
    for q in range(TEAM):
        hid_t[:, 128 * q : 128 * q + 128] = hid8[q].T

    for k in range(1, TEAM):
        i = lax.rem(p + k, TEAM)
        q = slot_of(i)
        arrival(tab8.at[q], tab_r.at[q], (base + i, r))
    tab8[me] = tab[...]
    to_scalars = pltpu.make_async_copy(tab8.at[r // 2], raw, loc.at[3])
    to_scalars.start()
    to_scalars.wait()

    def list_blocks(s, carry):
        for b in range(SEQ):
            users_of[b, s] = 64
        for j in range(4):
            name = raw[2 + j, s]
            found = 0
            for b in range(SEQ):
                hit = raw[0, b] == name
                found = jnp.where(hit, b, found)
                users_of[b, s] = jnp.where(hit, 4 * s + j, users_of[b, s])
            slots_of[s, j] = found
        return carry

    lax.fori_loop(0, SEQ, list_blocks, 0)

    lo = low_lanes((128, 128))
    zero = jnp.zeros((128, 128), BF)
    got_all(0)

    def probabilities(s):
        qz = jnp.where(lo, zero, pltpu.roll(land_qk[s], 64, 1)) * jnp.asarray(0.125, BF)
        count = raw[1, s]
        scores = [
            jnp.where(j < count, dot(land_qk[slots_of[s, j]], qz, NT), -1e30) for j in range(4)
        ]
        top = jnp.max(
            jnp.maximum(jnp.maximum(scores[0], scores[1]), jnp.maximum(scores[2], scores[3])),
            axis=0,
            keepdims=True,
        )
        expo = [jnp.exp(v - top) for v in scores]
        total = jnp.sum((expo[0] + expo[1]) + (expo[2] + expo[3]), axis=0, keepdims=True)
        inv = 1.0 / total
        for j in range(4):
            prob = expo[j] * inv
            probs[s, j] = prob
            lows[s, 128 * j : 128 * j + 128] = prob.astype(BF)

    def forward(g, carry):
        for n in range(4):
            probabilities(4 * g + n)
        return carry

    lax.fori_loop(0, 4, forward, 0)
    got_all(1)
    for s in range(SEQ):
        v_full[s, 0:64] = land_v[s]
        v_full[s, 64:128] = pltpu.roll(land_v[s], 64, 1)

    def blocks_of(g):
        return [lax.rem(r + 1 + 4 * g + n, SEQ) for n in range(4)]

    def hand_over(kind, g):
        for n, s in enumerate(blocks_of(g)):
            if n < 3:
                message(kind, s).start()
            else:

                @pl.when(s != r)
                def _():
                    message(kind, s).start()

    def attention(g, carry):
        for s in blocks_of(g):
            values = [v_full[slots_of[s, j]] for j in range(4)]
            attn = dot(jnp.concatenate(values, axis=0), lows[s], TN).T.astype(BF)
            back_a[s] = merge(attn[0:64], attn[64:128])
        hand_over(3, g)
        return carry

    lax.fori_loop(0, 4, attention, 0)
    keep(3)
    got_all(2)

    def gradients(s):
        qk, grad = land_qk[s], land_g[s]
        turned = pltpu.roll(grad, 64, 1)
        gz = jnp.where(lo, jnp.concatenate([grad, turned], axis=0), zero)
        gv = jnp.where(lo, zero, jnp.concatenate([turned, grad], axis=0))
        rhs = jnp.concatenate([jnp.where(lo, qk, zero), gv], axis=0)
        slots = [slots_of[s, j] for j in range(4)]
        keys = [land_qk[b] for b in slots]
        grad_p = [dot(v_full[b], gz, NT) for b in slots]
        prob = [probs[s, j] for j in range(4)]
        prod = [a * g for a, g in zip(prob, grad_p)]
        delta = jnp.sum((prod[0] + prod[1]) + (prod[2] + prod[3]), axis=0, keepdims=True)
        grad_s = [(a * (g - delta) * 0.125).astype(BF) for a, g in zip(prob, grad_p)]
        grad_q = dot(
            jnp.concatenate(keys, axis=0), jnp.concatenate(grad_s, axis=0), TN
        ).T.astype(BF)
        back_q[s] = merge_high(grad_q[0:64], grad_q[64:128])
        for j in range(4):
            low = lows[s, 128 * j : 128 * j + 128]
            tiles[4 * s + j] = dot(jnp.concatenate([grad_s[j], low], axis=1), rhs)

    def backward(g, carry):
        for s in blocks_of(g):
            gradients(s)
        hand_over(4, g)
        return carry

    lax.fori_loop(0, 4, backward, 0)
    keep(4)
    tiles[64] = jnp.zeros((128, 128), F32)

    def collect(n, carry):
        b = lax.rem(r + 1 + n, SEQ)
        total = tiles[users_of[b, 0]]
        for s in range(1, SEQ):
            total += tiles[users_of[b, s]]
        low = total.astype(BF)
        back_k[b] = merge(low[0:64], low[64:128])
        back_v[b] = merge_high(low[0:64], low[64:128])
        return carry

    lax.fori_loop(0, SEQ, collect, 0)

    give_all(5)

    def half_rows(core):
        return pl.ds(pl.multiple_of(core * HALF, HALF), HALF)

    def take(core, kind):
        for n in range(XS):
            i = core * XS + n
            a, b = targets[kind][2 * i], targets[kind][2 * i + 1]
            start = pl.multiple_of(i * ROWS, ROWS)
            cols = pl.ds(128 * (kind - 3), 128)
            mix[pl.ds(start, 64), cols] = merge(a, b)
            mix[pl.ds(start + 64, 64), cols] = merge_high(a, b)

    def product(core, n):
        if n == 0:
            return dot(mix[half_rows(core), 0:128], w_t[384:512, :])
        return dot(mix[half_rows(core), 128:512], w_t[0:384, :])

    def share(n):
        result = product(1 - c, n).astype(BF)
        for i in range(XS):
            part[n, i] = result[i * ROWS : i * ROWS + ROWS]
        for k in (1, 3, 2, 0):
            i = turn(k)
            sends.append(push(part.at[n, i], sib.at[n, i], sib_s.at[n, k], sib_r.at[n, i], sibling))

    def pass_on(n):
        result = product(c, n)
        for i in range(XS):
            total[i] = result[i * ROWS : i * ROWS + ROWS]
        for k in (1, 3, 2, 0):
            i = turn(k)
            arrival(sib.at[n, i], sib_r.at[n, i], sibling)
            part[n, XS + i] = (total[i] + sib[n, i].astype(F32)).astype(BF)
            if k:
                sends.append(
                    push(part.at[n, XS + i], far.at[n, x], far_s.at[n, k], far_r.at[n, x], at_x(k))
                )

    def result_of(n, first):
        result = first.astype(F32) + part[n, XS + x].astype(F32)
        for k in NEAR:
            arrival(far.at[n, turn(k)], far_r.at[n, turn(k)], at_x(k))
            result += far[n, turn(k)].astype(F32)
        return result.astype(BF)

    terms = (terms_a, terms_k, terms_v)
    from_y = (from_y_a, from_y_k, from_y_v)
    to_z = (to_z_a, to_z_k, to_z_v)
    from_z = (from_z_a, from_z_k, from_z_v)
    full = (full_a, full_k, full_v)

    def terms_out(g):
        if g == 0:
            cots = cot8[...].reshape(TEAM * ROWS, WIDTH)
            out_term = dot(mix[:, 0:128], cots, TN).astype(BF)
            for j in range(TEAM):
                block = out_term[:, 128 * j : 128 * j + 128]
                terms_a[2 * j, :, 128:256] = block[0:64]
                terms_a[2 * j + 1, :, 128:256] = block[64:128]
        first = 128 * (g + 1)
        for h in range(4):
            rows = hid_t[256 * h : 256 * h + 256]
            in_term = dot(rows, mix[:, first : first + 128]).astype(BF)
            for m in range(YS):
                terms[g][4 * h + m, :, 0:128] = in_term[64 * m : 64 * m + 64]
            for k in NEAR:
                sends.append(
                    push(
                        terms[g].at[4 * h + lax.rem(y + k, YS)], from_y[g].at[y, h],
                        y_s.at[g, k, h], y_r.at[g, y, h], (dp, at_y(k)),
                    )
                )

    def half_of(side):
        return pl.ds(pl.multiple_of(side * 32, 32), 32)

    def along_z(g):
        for k in (2, 1, 3, 0):
            h = lax.rem(zh + k, 4)
            result = terms[g][4 * h + y].astype(F32)
            for m in NEAR:
                t = lax.rem(y + m, YS)
                arrival(from_y[g].at[t, h], y_r.at[g, t, h], (dp, at_y(m)))
                result += from_y[g][t, h].astype(F32)
            to_z[g][h] = result.astype(BF)
            for other in (0, 1):
                if k or other:
                    side = lax.rem(zl + other, 2)
                    where = across if other else dp
                    sends.append(
                        push(
                            to_z[g].at[h, half_of(side)], from_z[g].at[zl, zh],
                            z_s.at[g, other, h], z_r.at[g, zl, zh], (where, h * YS + y),
                        )
                    )

    def to_team(g):
        result = to_z[g][zh, half_of(zl)].astype(F32)
        for k in (1, 3, 2, 0):
            h = lax.rem(zh + k, 4)
            for other in (0, 1):
                if k or other:
                    side = lax.rem(zl + other, 2)
                    arrival(from_z[g].at[side, h], z_r.at[g, side, h], (dp, at_z(k)))
                    result += from_z[g][side, h].astype(F32)
        piece = full[g].at[me, half_of(zl)]
        piece[...] = result.astype(BF)
        for k in range(1, 2 * TEAM):
            where = lax.rem(dp + k, 2 * TEAM)
            sends.append(push(piece, piece, g_s.at[g, k], g_r.at[g, zl, me], (where, r)))

    def from_team(g):
        for k in range(1, 2 * TEAM):
            other = lax.rem(dp + k, 2 * TEAM)
            side, q = other // TEAM, slot_of(other % TEAM)
            arrival(full[g].at[q, half_of(side)], g_r.at[g, side, q], (other, r))

    def out_piece(i):
        t = 2 * i + r % 2
        src = full_a.at[(i % 2) * XS + i // 2, :, 128:256]
        return t, remote(src, wob.at[r // 2], q_s.at[i], q_r.at[r // 2], (dp, t))

    def write(g):
        for i in range(TEAM):
            q = (i % 2) * XS + i // 2
            proj_grad[:, g, 128 * i : 128 * i + 128] = full[g][q, :, 0:128].astype(F32)

    def take_all(kind):
        take(0, kind)
        take(1, kind)

    got_all(3)
    take_all(3)
    share(0)
    pass_on(0)
    give_all(6)
    got_all(4)
    take_all(4)
    terms_out(0)
    got_all(5)
    take_all(5)
    terms_out(1)
    along_z(0)
    got_all(6)
    take_all(6)
    terms_out(2)
    share(1)
    to_team(0)
    along_z(1)
    pass_on(1)
    to_team(1)
    along_z(2)
    layer_out[...] = result_of(0, hid8[me])
    from_team(0)
    for i in range(TEAM):
        t, copy = out_piece(i)

        @pl.when(t != r)
        def _():
            copy.start()

        @pl.when(t == r)
        def _():
            wob[r // 2] = full_a[(i % 2) * XS + i // 2, :, 128:256]

    write(0)
    to_team(2)
    from_team(1)
    write(1)
    for j in range(TEAM):
        t, copy = out_piece(j)

        @pl.when(t != r)
        def _():
            arrival(wob.at[j], q_r.at[j], (dp, t))
            copy.wait_send()

        proj_grad[:, 3, 128 * j : 128 * j + 128] = wob[j].astype(F32)
    features_grad[...] = result_of(1, cot8[me])
    from_team(2)
    write(2)

    for copy in sends:
        copy.wait_send()

    @pl.when(spread)
    def _():
        for j in range(TEAM):
            t = 2 * j + r % 2

            @pl.when(t != r)
            def _():
                remote(
                    wt.at[j, :, 384:512], out_part(t), sc_s.at[j], sc_r, (dp, t)
                ).wait_send()

    def sent(k, carry):
        t = lax.rem(r + k, SEQ)
        for kind in range(7):
            message(kind, t).wait_send()
        return carry

    lax.fori_loop(1, SEQ, sent, 0)


def layer(feat, labels, table, order, neigh, counts, cot, wt):
    vmem = pl.BlockSpec(memory_space=pltpu.VMEM)
    dma = pltpu.SemaphoreType.DMA
    tile, small = (128, 128), (64, 128)
    act = (ROWS, WIDTH)
    widths = (256, 128, 128)
    return pl.pallas_call(
        kernel,
        out_shape=[
            jax.ShapeDtypeStruct(act, BF),
            jax.ShapeDtypeStruct(act, BF),
            jax.ShapeDtypeStruct((SHARD, 4, WIDTH), F32),
        ],
        in_specs=[vmem] * 8,
        out_specs=[vmem] * 3,
        scratch_shapes=[
            pltpu.VMEM(act, BF),
            pltpu.VMEM((8, 128), jnp.int32),
            pltpu.VMEM((TEAM, *act), BF),
            pltpu.VMEM((TEAM, *act), BF),
            pltpu.VMEM((WIDTH, TEAM * ROWS), BF),
            pltpu.VMEM((WIDTH, 512), BF),
            pltpu.VMEM((WIDTH, 128), BF),
            pltpu.VMEM((512, WIDTH), BF),
            pltpu.VMEM((TEAM, 8, 128), jnp.int32),
            pltpu.SMEM((8, 128), jnp.int32),
            pltpu.SMEM((SEQ, 4), jnp.int32),
            pltpu.SMEM((SEQ, SEQ), jnp.int32),
            pltpu.VMEM((SEQ, *tile), BF),
            pltpu.VMEM((SEQ, *small), BF),
            pltpu.VMEM((SEQ, *small), BF),
            pltpu.VMEM((SEQ, *tile), BF),
            pltpu.VMEM((SEQ, *small), BF),
            pltpu.VMEM((SEQ, *small), BF),
            pltpu.VMEM((SEQ, *tile), BF),
            pltpu.VMEM((SEQ, 4, *tile), F32),
            pltpu.VMEM((SEQ, 512, 128), BF),
            pltpu.VMEM((SEQ * 4 + 1, *tile), F32),
            *[pltpu.VMEM((SEQ, *small), BF)] * 8,
            pltpu.VMEM((TEAM * ROWS, 512), BF),
            pltpu.VMEM((2, 2 * XS, *act), BF),
            pltpu.VMEM((XS, *act), F32),
            pltpu.VMEM((2, XS, *act), BF),
            pltpu.VMEM((2, XS, *act), BF),
            *[pltpu.VMEM((SEQ, SHARD, w), BF) for w in widths],
            *[pltpu.VMEM((YS, 4, SHARD, w), BF) for w in widths],
            *[pltpu.VMEM((4, SHARD, w), BF) for w in widths],
            *[pltpu.VMEM((2, 4, SHARD // 2, w), BF) for w in widths],
            *[pltpu.VMEM((TEAM, SHARD, w), BF) for w in widths],
            pltpu.VMEM((TEAM, SHARD, 128), BF),
            dma((8,)), dma((8,)), dma((2,)), dma((8,)), dma((8,)), dma((2,)), dma((8,)), dma((8,)),
            dma((17,)), dma((16,)), dma((17,)), dma((16,)), dma((17,)), dma((16,)), dma((8,)), dma(()),
            dma((7, 16)), dma((7, 16)),
            dma((2, 4)), dma((2, 4)), dma((2, 4)), dma((2, 4)), dma((3, 4, 4)), dma((3, 4, 4)),
            dma((3, 2, 4)), dma((3, 2, 4)), dma((3, 16)), dma((3, 2, 8)), dma((8,)), dma((8,)), dma((4,)),
        ],
        compiler_params=pltpu.CompilerParams(
            collective_id=1, has_side_effects=True, vmem_limit_bytes=VMEM_BYTES
        ),
    )(feat, labels, table, order, neigh, counts, cot, wt)


def per_device(
    features, labels, label_table, proj_weight, block_order, neighbours, counts, cotangent
):
    wt = proj_weight.reshape(SHARD, 4, TEAM, 128).transpose(2, 0, 1, 3).reshape(TEAM, SHARD, 512)
    layer_out, features_grad, proj_grad = layer(
        features[0], labels, label_table, block_order, neighbours[0].T, counts, cotangent[0], wt
    )
    return (layer_out[None], features_grad[None], proj_grad)


def solution(mesh):
    placed = (
        P("dp", "seq", None),
        P("dp", "seq"),
        P(),
        P("seq", None, None),
        P("dp", None),
        P("dp", None, None),
        P("dp", None),
        P("dp", "seq", None),
    )
    return jax.shard_map(
        per_device,
        mesh=mesh,
        in_specs=placed,
        out_specs=(P("dp", "seq", None), P("dp", "seq", None), P("seq", None, None)),
        check_vma=False,
    )
```

```python
import jax
import jax.numpy as jnp
from jax import lax
from jax.experimental import pallas as pl
from jax.experimental.pallas import tpu as pltpu
from jax.sharding import PartitionSpec as P

XS, YS, TEAM, SEQ, ROWS, WIDTH = 4, 4, 8, 16, 128, 1024
SHARD = WIDTH // SEQ
HALF = 4 * ROWS
BF, F32 = jnp.bfloat16, jnp.float32
NN = (((1,), (0,)), ((), ()))
NT = (((1,), (1,)), ((), ()))
TN = (((0,), (0,)), ((), ()))
VMEM_BYTES = 40 << 20
MESH = pl.DeviceIdType.MESH
NEAR = (1, 3, 2)


def dot(a, b, dims=NN):
    return lax.dot_general(a, b, dims, preferred_element_type=F32)


def remote(src, dst, send, recv, where):
    return pltpu.make_async_remote_copy(
        src_ref=src, dst_ref=dst, send_sem=send, recv_sem=recv, device_id=where, device_id_type=MESH
    )


def push(src, dst, send, recv, where):
    copy = remote(src, dst, send, recv, where)
    copy.start()
    return copy


def arrival(dst, recv, where):
    remote(dst, dst, recv, recv, where).wait_recv()


def low_lanes(shape):
    return lax.broadcasted_iota(jnp.int32, shape, 1) < 64


def merge(a, b):
    return jnp.where(low_lanes(a.shape), a, pltpu.roll(b, 64, 1))


def merge_high(a, b):
    return jnp.where(low_lanes(a.shape), pltpu.roll(a, 64, 1), b)


def kernel(
    feat, labels, table, order, neigh, counts, cot, wt,
    layer_out, features_grad, proj_grad,
    hid, tab, hid8, cot8, hid_t, wg, wo, w_t, tab8, raw, slots_of, users_of, stage_qk, stage_v, stage_g, land_qk, land_v, land_g,
    v_full, probs, lows, tiles, back_a, back_q, back_k, back_v, home_a, home_q, home_k, home_v, mix,
    part, total, sib, far, terms_o, terms_q, terms_kv, from_y_o, from_y_q, from_y_kv,
    to_z_o, to_z_q, to_z_kv, from_z_o, from_z_q, from_z_kv, full_o, full_q, full_kv, wob,
    hid_s, hid_r, hid_h, cot_s, cot_r, cot_h, tab_s, tab_r, w_s, w_r, v_s, v_r, o_s, o_r, sc_s, sc_r,
    m_s, m_r, sib_s, sib_r, far_s, far_r, y_s, y_r, z_s, z_r, g_s, g_r, q_s, q_r, loc,
):
    dp, r = lax.axis_index("dp"), lax.axis_index("seq")
    zl, p = dp // TEAM, dp % TEAM
    x, c = p // 2, p % 2
    zh, y = r // YS, r % YS
    base = zl * TEAM
    me = c * XS + x
    sibling = (base + x * 2 + 1 - c, r)
    across = lax.rem(dp + TEAM, 2 * TEAM)

    def turn(k):
        return lax.rem(x + k, XS)

    def slot(k):
        return c * XS + turn(k)

    def at_x(k):
        return (base + turn(k) * 2 + c, r)

    def at_z(k):
        return lax.rem(zh + k, 4) * YS + y

    def at_y(k):
        return zh * YS + lax.rem(y + k, YS)

    def team_peer(k):
        return base + lax.rem(p + k, TEAM)

    def slot_of(q):
        return lax.rem(q, 2) * XS + q // 2

    barrier = pltpu.get_barrier_semaphore()
    greeted = [(lax.rem(dp + k, 2 * TEAM), r) for k in range(1, 2 * TEAM)]
    greeted += [(dp, lax.rem(r + k, SEQ)) for k in range(1, SEQ)]
    greeted += [(across, at_z(k)) for k in (1, 2, 3)]
    for where in greeted:
        pl.semaphore_signal(barrier, inc=1, device_id=where, device_id_type=MESH)
    chosen = lax.broadcasted_iota(jnp.int32, (table.shape[0], ROWS), 0) == labels[...]
    embedded = dot(chosen.astype(F32).astype(BF), table[...], TN)
    hid[...] = (feat[...].astype(F32) + embedded).astype(BF)
    tab[...] = jnp.zeros_like(tab)
    tab[0:1, 0:SEQ] = order[...]
    tab[1:2, 0:SEQ] = counts[...]
    tab[2:6, 0:SEQ] = neigh[...]
    pl.semaphore_wait(barrier, len(greeted))
    sends = []

    sources = (stage_qk, stage_v, stage_g, back_a, back_q, back_k, back_v)
    targets = (land_qk, land_v, land_g, home_a, home_q, home_k, home_v)

    def message(kind, t):
        return remote(
            sources[kind].at[t], targets[kind].at[r], m_s.at[kind, t], m_r.at[kind, r], (dp, t)
        )

    def after(k):
        return lax.rem(r + k, SEQ)

    def before(k):
        return lax.rem(r + SEQ - k, SEQ)

    def keep(kind):
        targets[kind][r] = sources[kind][r]

    def arrived(kind, t):
        arrival(targets[kind].at[t], m_r.at[kind, t], (dp, t))

    def give_all(kind):
        def one(k, carry):
            message(kind, after(k)).start()
            return carry

        lax.fori_loop(1, SEQ, one, 0)
        keep(kind)

    def got_all(kind):
        def one(k, carry):
            arrived(kind, before(k))
            return carry

        lax.fori_loop(1, SEQ, one, 0)

    halves = (pl.ds(0, 64), pl.ds(64, 64))

    def spread_x(array, own, send, recv):
        for k in (1, 3):
            sends.append(push(own, array.at[me], send.at[k], recv.at[me], at_x(k)))
        sends.append(push(own, array.at[me], send.at[0], recv.at[me], sibling))

    def forward_x(array, send, recv, opposite):
        for k in (1, 3):
            q = slot(k)
            arrival(array.at[q], recv.at[q], at_x(k))
            h = k // 3
            piece = array.at[q, halves[h]]
            sends.append(push(piece, piece, send.at[4 + k], opposite.at[h], at_x(4 - k)))
            sends.append(push(array.at[q], array.at[q], send.at[1 + k], recv.at[q], sibling))

    def finish_x(array, send, recv, opposite):
        q = slot(2)
        for h, k in ((0, 1), (1, 3)):
            arrival(array.at[q, halves[h]], opposite.at[h], at_x(k))
        sends.append(push(array.at[q], array.at[q], send.at[6], recv.at[q], sibling))

    def other_core(array, recv):
        for k in range(XS):
            q = (1 - c) * XS + turn(k)
            arrival(array.at[q], recv.at[q], sibling)

    def rows_of(s):
        return pl.ds(pl.multiple_of(s * SHARD, SHARD), SHARD)

    def qk_part(s):
        return wg.at[rows_of(s), 0:256]

    def v_part(s):
        return wg.at[rows_of(s), 256:384]

    def out_part(s):
        return wg.at[rows_of(s), 384:512]

    own_w = pltpu.make_async_copy(wt.at[p, :, 0:384], wg.at[rows_of(r), 0:384], loc.at[0])
    own_w.start()
    mine_qk, mine_v = wt.at[p, :, 0:256], wt.at[p, :, 256:384]
    for k in NEAR:
        sends.append(push(mine_qk, qk_part(r), w_s.at[k], w_r.at[r], (dp, at_z(k))))
    for k in NEAR:
        sends.append(push(mine_qk, qk_part(r), w_s.at[3 + k], w_r.at[r], (dp, at_y(k))))
    for k in NEAR:
        sends.append(push(mine_v, v_part(r), v_s.at[k], v_r.at[r], (dp, at_z(k))))
    for k in NEAR:
        sends.append(push(mine_v, v_part(r), v_s.at[3 + k], v_r.at[r], (dp, at_y(k))))

    spread = r // 2 == p

    @pl.when(spread)
    def _():
        for j in range(TEAM):
            t = 2 * j + r % 2

            @pl.when(t != r)
            def _():
                push(wt.at[j, :, 384:512], out_part(t), sc_s.at[j], sc_r, (dp, t))

    keep_hid = pltpu.make_async_copy(hid, hid8.at[me], loc.at[1])
    keep_hid.start()
    keep_cot = pltpu.make_async_copy(cot, cot8.at[me], loc.at[2])
    keep_cot.start()
    spread_x(hid8, hid, hid_s, hid_r)
    for k in range(1, TEAM):
        sends.append(push(tab, tab8.at[me], tab_s.at[k], tab_r.at[me], (team_peer(k), r)))

    for n, k in enumerate(NEAR):
        s = at_z(k)
        arrival(qk_part(s), w_r.at[s], (dp, s))
        for m in NEAR:
            sends.append(
                push(qk_part(s), qk_part(s), w_s.at[7 + n * 3 + m], w_r.at[s], (dp, at_y(m)))
            )

    forward_x(hid8, hid_s, hid_r, hid_h)
    spread_x(cot8, cot, cot_s, cot_r)
    for n, k in enumerate(NEAR):
        s = at_z(k)
        arrival(v_part(s), v_r.at[s], (dp, s))
        for m in NEAR:
            sends.append(
                push(v_part(s), v_part(s), v_s.at[7 + n * 3 + m], v_r.at[s], (dp, at_y(m)))
            )

    piece = out_part(r)

    @pl.when(spread)
    def _():
        copy = pltpu.make_async_copy(wt.at[p, :, 384:512], piece, loc.at[3])
        copy.start()
        copy.wait()

    @pl.when(jnp.logical_not(spread))
    def _():
        arrival(piece, sc_r, (dp, r))

    for k in NEAR:
        sends.append(push(piece, piece, o_s.at[k], o_r.at[r], (dp, at_z(k))))
    for k in NEAR:
        sends.append(push(piece, piece, o_s.at[3 + k], o_r.at[r], (dp, at_y(k))))
    finish_x(hid8, hid_s, hid_r, hid_h)
    for n, k in enumerate(NEAR):
        s = at_z(k)
        arrival(out_part(s), o_r.at[s], (dp, s))
        for m in NEAR:
            sends.append(
                push(out_part(s), out_part(s), o_s.at[7 + n * 3 + m], o_r.at[s], (dp, at_y(m)))
            )

    def from_all_y(piece_of, sems):
        for m in NEAR:
            for k in range(4):
                s = lax.rem(zh + k, 4) * YS + lax.rem(y + m, YS)
                arrival(piece_of(s), sems.at[s], (dp, s))

    def group_rows(array, core):
        block = array[pl.ds(pl.multiple_of(core * XS, XS), XS)]
        return block.reshape(HALF, array.shape[2])

    def packed(stage, core, result):
        for n in range(XS):
            top = result[n * ROWS : n * ROWS + 64]
            bottom = result[n * ROWS + 64 : n * ROWS + ROWS]
            i = core * XS + n
            stage[2 * i] = merge(top, bottom)
            stage[2 * i + 1] = merge_high(top, bottom)

    from_all_y(qk_part, w_r)
    own_w.wait()
    keep_hid.wait()
    for core in (c, 1 - c):
        if core is not c:
            other_core(hid8, hid_r)
        queries_keys = dot(group_rows(hid8, core), wg[:, 0:256]).astype(BF)
        for n in range(XS):
            rows = queries_keys[n * ROWS : n * ROWS + ROWS]
            q, k = rows[:, 0:128], rows[:, 128:256]
            i = core * XS + n
            stage_qk[2 * i] = merge(q, k)
            stage_qk[2 * i + 1] = merge_high(q, k)
    give_all(0)

    forward_x(cot8, cot_s, cot_r, cot_h)
    from_all_y(v_part, v_r)
    for core in (c, 1 - c):
        packed(stage_v, core, dot(group_rows(hid8, core), wg[:, 256:384]).astype(BF))
    give_all(1)
    from_all_y(out_part, o_r)
    for j in range(TEAM):
        block = wg[128 * j : 128 * j + 128, 384:512]
        wo[128 * j : 128 * j + 128, :] = block.T
        w_t[384:512, 128 * j : 128 * j + 128] = block
    finish_x(cot8, cot_s, cot_r, cot_h)
    keep_cot.wait()
    for core in (c, 1 - c):
        if core is not c:
            other_core(cot8, cot_r)
        packed(stage_g, core, dot(group_rows(cot8, core), wo[...]).astype(BF))

    give_all(2)

    for n in range(3):
        w_t[128 * n : 128 * n + 128, :] = wg[:, 128 * n : 128 * n + 128].T
    for q in range(TEAM):
        hid_t[:, 128 * q : 128 * q + 128] = hid8[q].T

    for k in range(1, TEAM):
        i = lax.rem(p + k, TEAM)
        q = slot_of(i)
        arrival(tab8.at[q], tab_r.at[q], (base + i, r))
    tab8[me] = tab[...]
    to_scalars = pltpu.make_async_copy(tab8.at[r // 2], raw, loc.at[3])
    to_scalars.start()
    to_scalars.wait()

    def list_blocks(s, carry):
        for b in range(SEQ):
            users_of[b, s] = 64
        for j in range(4):
            name = raw[2 + j, s]
            found = 0
            for b in range(SEQ):
                hit = raw[0, b] == name
                found = jnp.where(hit, b, found)
                users_of[b, s] = jnp.where(hit, 4 * s + j, users_of[b, s])
            slots_of[s, j] = found
        return carry

    lax.fori_loop(0, SEQ, list_blocks, 0)

    lo = low_lanes((128, 128))
    zero = jnp.zeros((128, 128), BF)
    got_all(0)

    def probabilities(s):
        qz = jnp.where(lo, zero, pltpu.roll(land_qk[s], 64, 1)) * jnp.asarray(0.125, BF)
        count = raw[1, s]
        scores = [
            jnp.where(j < count, dot(land_qk[slots_of[s, j]], qz, NT), -1e30) for j in range(4)
        ]
        top = jnp.max(
            jnp.maximum(jnp.maximum(scores[0], scores[1]), jnp.maximum(scores[2], scores[3])),
            axis=0,
            keepdims=True,
        )
        expo = [jnp.exp(v - top) for v in scores]
        total = jnp.sum((expo[0] + expo[1]) + (expo[2] + expo[3]), axis=0, keepdims=True)
        inv = 1.0 / total
        for j in range(4):
            prob = expo[j] * inv
            probs[s, j] = prob
            lows[s, 128 * j : 128 * j + 128] = prob.astype(BF)

    def forward(g, carry):
        for n in range(4):
            probabilities(4 * g + n)
        return carry

    lax.fori_loop(0, 4, forward, 0)
    got_all(1)
    for s in range(SEQ):
        v_full[s, 0:64] = land_v[s]
        v_full[s, 64:128] = pltpu.roll(land_v[s], 64, 1)

    def blocks_of(g):
        return [lax.rem(r + 1 + 4 * g + n, SEQ) for n in range(4)]

    def hand_over(kind, g):
        for n, s in enumerate(blocks_of(g)):
            if n < 3:
                message(kind, s).start()
            else:

                @pl.when(s != r)
                def _():
                    message(kind, s).start()

    def attention(g, carry):
        for s in blocks_of(g):
            values = [v_full[slots_of[s, j]] for j in range(4)]
            attn = dot(jnp.concatenate(values, axis=0), lows[s], TN).T.astype(BF)
            back_a[s] = merge(attn[0:64], attn[64:128])
        hand_over(3, g)
        return carry

    lax.fori_loop(0, 4, attention, 0)
    keep(3)
    got_all(2)

    def gradients(s):
        qk, grad = land_qk[s], land_g[s]
        turned = pltpu.roll(grad, 64, 1)
        gz = jnp.where(lo, jnp.concatenate([grad, turned], axis=0), zero)
        gv = jnp.where(lo, zero, jnp.concatenate([turned, grad], axis=0))
        rhs = jnp.concatenate([jnp.where(lo, qk, zero), gv], axis=0)
        slots = [slots_of[s, j] for j in range(4)]
        keys = [land_qk[b] for b in slots]
        grad_p = [dot(v_full[b], gz, NT) for b in slots]
        prob = [probs[s, j] for j in range(4)]
        prod = [a * g for a, g in zip(prob, grad_p)]
        delta = jnp.sum((prod[0] + prod[1]) + (prod[2] + prod[3]), axis=0, keepdims=True)
        grad_s = [(a * (g - delta) * 0.125).astype(BF) for a, g in zip(prob, grad_p)]
        grad_q = dot(
            jnp.concatenate(keys, axis=0), jnp.concatenate(grad_s, axis=0), TN
        ).T.astype(BF)
        back_q[s] = merge_high(grad_q[0:64], grad_q[64:128])
        for j in range(4):
            low = lows[s, 128 * j : 128 * j + 128]
            tiles[4 * s + j] = dot(jnp.concatenate([grad_s[j], low], axis=1), rhs)

    def backward(g, carry):
        for s in blocks_of(g):
            gradients(s)
        hand_over(4, g)
        return carry

    lax.fori_loop(0, 4, backward, 0)
    keep(4)
    tiles[64] = jnp.zeros((128, 128), F32)

    def collect(n, carry):
        b = lax.rem(r + 1 + n, SEQ)
        total = tiles[users_of[b, 0]]
        for s in range(1, SEQ):
            total += tiles[users_of[b, s]]
        low = total.astype(BF)
        back_k[b] = merge(low[0:64], low[64:128])
        back_v[b] = merge_high(low[0:64], low[64:128])

        @pl.when(n < SEQ - 1)
        def _():
            message(5, b).start()
            message(6, b).start()

        return carry

    lax.fori_loop(0, SEQ, collect, 0)
    keep(5)
    keep(6)

    def half_rows(core):
        return pl.ds(pl.multiple_of(core * HALF, HALF), HALF)

    def take(core, kind):
        for n in range(XS):
            i = core * XS + n
            a, b = targets[kind][2 * i], targets[kind][2 * i + 1]
            start = pl.multiple_of(i * ROWS, ROWS)
            cols = pl.ds(128 * (kind - 3), 128)
            mix[pl.ds(start, 64), cols] = merge(a, b)
            mix[pl.ds(start + 64, 64), cols] = merge_high(a, b)

    def product(core, n):
        if n == 0:
            return dot(mix[half_rows(core), 0:128], w_t[384:512, :])
        return dot(mix[half_rows(core), 128:512], w_t[0:384, :])

    def share(n):
        result = product(1 - c, n).astype(BF)
        for i in range(XS):
            part[n, i] = result[i * ROWS : i * ROWS + ROWS]
        for k in (1, 3, 2, 0):
            i = turn(k)
            sends.append(push(part.at[n, i], sib.at[n, i], sib_s.at[n, k], sib_r.at[n, i], sibling))

    def pass_on(n):
        result = product(c, n)
        for i in range(XS):
            total[i] = result[i * ROWS : i * ROWS + ROWS]
        for k in (1, 3, 2, 0):
            i = turn(k)
            arrival(sib.at[n, i], sib_r.at[n, i], sibling)
            part[n, XS + i] = (total[i] + sib[n, i].astype(F32)).astype(BF)
            if k:
                sends.append(
                    push(part.at[n, XS + i], far.at[n, x], far_s.at[n, k], far_r.at[n, x], at_x(k))
                )

    def result_of(n, first):
        result = first.astype(F32) + part[n, XS + x].astype(F32)
        for k in NEAR:
            arrival(far.at[n, turn(k)], far_r.at[n, turn(k)], at_x(k))
            result += far[n, turn(k)].astype(F32)
        return result.astype(BF)

    terms = (terms_o, terms_q, terms_kv)
    from_y = (from_y_o, from_y_q, from_y_kv)
    to_z = (to_z_o, to_z_q, to_z_kv)
    from_z = (from_z_o, from_z_q, from_z_kv)
    full = (full_o, full_q, full_kv)

    def terms_out(g):
        if g == 0:
            cots = cot8[...].reshape(TEAM * ROWS, WIDTH)
            out_term = dot(mix[:, 0:128], cots, TN).astype(BF)
            for j in range(TEAM):
                block = out_term[:, 128 * j : 128 * j + 128]
                terms_o[2 * j] = block[0:64]
                terms_o[2 * j + 1] = block[64:128]
        for h in range(4):
            if g:
                cols = mix[:, 128 * g : 256 * g]
                in_term = dot(hid_t[256 * h : 256 * h + 256], cols).astype(BF)
                for m in range(YS):
                    terms[g][4 * h + m] = in_term[64 * m : 64 * m + 64]
            for k in NEAR:
                sends.append(
                    push(
                        terms[g].at[4 * h + lax.rem(y + k, YS)], from_y[g].at[y, h],
                        y_s.at[g, k, h], y_r.at[g, y, h], (dp, at_y(k)),
                    )
                )

    def half_of(side):
        return pl.ds(pl.multiple_of(side * 32, 32), 32)

    def along_z(g):
        for k in (2, 1, 3, 0):
            h = lax.rem(zh + k, 4)
            result = terms[g][4 * h + y].astype(F32)
            for m in NEAR:
                t = lax.rem(y + m, YS)
                arrival(from_y[g].at[t, h], y_r.at[g, t, h], (dp, at_y(m)))
                result += from_y[g][t, h].astype(F32)
            to_z[g][h] = result.astype(BF)
            for other in (0, 1):
                if k or other:
                    side = lax.rem(zl + other, 2)
                    where = across if other else dp
                    sends.append(
                        push(
                            to_z[g].at[h, half_of(side)], from_z[g].at[zl, zh],
                            z_s.at[g, other, h], z_r.at[g, zl, zh], (where, h * YS + y),
                        )
                    )

    def to_team(g):
        result = to_z[g][zh, half_of(zl)].astype(F32)
        for k in (1, 3, 2, 0):
            h = lax.rem(zh + k, 4)
            for other in (0, 1):
                if k or other:
                    side = lax.rem(zl + other, 2)
                    arrival(from_z[g].at[side, h], z_r.at[g, side, h], (dp, at_z(k)))
                    result += from_z[g][side, h].astype(F32)
        piece = full[g].at[me, half_of(zl)]
        piece[...] = result.astype(BF)
        for k in range(1, 2 * TEAM):
            where = lax.rem(dp + k, 2 * TEAM)
            sends.append(push(piece, piece, g_s.at[g, k], g_r.at[g, zl, me], (where, r)))

    def from_team(g):
        for k in range(1, 2 * TEAM):
            other = lax.rem(dp + k, 2 * TEAM)
            side, q = other // TEAM, slot_of(other % TEAM)
            arrival(full[g].at[q, half_of(side)], g_r.at[g, side, q], (other, r))

    def out_piece(i):
        t = 2 * i + r % 2
        src = full_o.at[(i % 2) * XS + i // 2]
        return t, remote(src, wob.at[r // 2], q_s.at[i], q_r.at[r // 2], (dp, t))

    def write(n, source, first):
        for i in range(TEAM):
            q = (i % 2) * XS + i // 2
            piece = source[q, :, first : first + 128]
            proj_grad[:, n, 128 * i : 128 * i + 128] = piece.astype(F32)

    def take_all(kind):
        take(0, kind)
        take(1, kind)

    got_all(3)
    take_all(3)
    share(0)
    terms_out(0)
    pass_on(0)
    got_all(4)
    take_all(4)
    terms_out(1)
    along_z(0)
    got_all(5)
    take_all(5)
    got_all(6)
    take_all(6)
    terms_out(2)
    share(1)
    to_team(0)
    along_z(1)
    pass_on(1)
    from_team(0)
    for i in range(TEAM):
        t, copy = out_piece(i)

        @pl.when(t != r)
        def _():
            copy.start()

        @pl.when(t == r)
        def _():
            wob[r // 2] = full_o[(i % 2) * XS + i // 2]

    to_team(1)
    along_z(2)
    layer_out[...] = result_of(0, hid8[me])
    from_team(1)
    write(0, full_q, 0)
    for j in range(TEAM):
        t, copy = out_piece(j)

        @pl.when(t != r)
        def _():
            arrival(wob.at[j], q_r.at[j], (dp, t))
            copy.wait_send()

        proj_grad[:, 3, 128 * j : 128 * j + 128] = wob[j].astype(F32)
    to_team(2)
    features_grad[...] = result_of(1, cot8[me])
    from_team(2)
    write(1, full_kv, 0)
    write(2, full_kv, 128)

    for copy in sends:
        copy.wait_send()

    @pl.when(spread)
    def _():
        for j in range(TEAM):
            t = 2 * j + r % 2

            @pl.when(t != r)
            def _():
                remote(
                    wt.at[j, :, 384:512], out_part(t), sc_s.at[j], sc_r, (dp, t)
                ).wait_send()

    def sent(k, carry):
        t = lax.rem(r + k, SEQ)
        for kind in range(7):
            message(kind, t).wait_send()
        return carry

    lax.fori_loop(1, SEQ, sent, 0)


def layer(feat, labels, table, order, neigh, counts, cot, wt):
    vmem = pl.BlockSpec(memory_space=pltpu.VMEM)
    dma = pltpu.SemaphoreType.DMA
    tile, small = (128, 128), (64, 128)
    act = (ROWS, WIDTH)
    widths = (128, 128, 256)
    return pl.pallas_call(
        kernel,
        out_shape=[
            jax.ShapeDtypeStruct(act, BF),
            jax.ShapeDtypeStruct(act, BF),
            jax.ShapeDtypeStruct((SHARD, 4, WIDTH), F32),
        ],
        in_specs=[vmem] * 6 + [pl.BlockSpec(memory_space=pl.ANY), vmem],
        out_specs=[vmem] * 3,
        scratch_shapes=[
            pltpu.VMEM(act, BF),
            pltpu.VMEM((8, 128), jnp.int32),
            pltpu.VMEM((TEAM, *act), BF),
            pltpu.VMEM((TEAM, *act), BF),
            pltpu.VMEM((WIDTH, TEAM * ROWS), BF),
            pltpu.VMEM((WIDTH, 512), BF),
            pltpu.VMEM((WIDTH, 128), BF),
            pltpu.VMEM((512, WIDTH), BF),
            pltpu.VMEM((TEAM, 8, 128), jnp.int32),
            pltpu.SMEM((8, 128), jnp.int32),
            pltpu.SMEM((SEQ, 4), jnp.int32),
            pltpu.SMEM((SEQ, SEQ), jnp.int32),
            pltpu.VMEM((SEQ, *tile), BF),
            pltpu.VMEM((SEQ, *small), BF),
            pltpu.VMEM((SEQ, *small), BF),
            pltpu.VMEM((SEQ, *tile), BF),
            pltpu.VMEM((SEQ, *small), BF),
            pltpu.VMEM((SEQ, *small), BF),
            pltpu.VMEM((SEQ, *tile), BF),
            pltpu.VMEM((SEQ, 4, *tile), F32),
            pltpu.VMEM((SEQ, 512, 128), BF),
            pltpu.VMEM((SEQ * 4 + 1, *tile), F32),
            *[pltpu.VMEM((SEQ, *small), BF)] * 8,
            pltpu.VMEM((TEAM * ROWS, 512), BF),
            pltpu.VMEM((2, 2 * XS, *act), BF),
            pltpu.VMEM((XS, *act), F32),
            pltpu.VMEM((2, XS, *act), BF),
            pltpu.VMEM((2, XS, *act), BF),
            *[pltpu.VMEM((SEQ, SHARD, w), BF) for w in widths],
            *[pltpu.VMEM((YS, 4, SHARD, w), BF) for w in widths],
            *[pltpu.VMEM((4, SHARD, w), BF) for w in widths],
            *[pltpu.VMEM((2, 4, SHARD // 2, w), BF) for w in widths],
            *[pltpu.VMEM((TEAM, SHARD, w), BF) for w in widths],
            pltpu.VMEM((TEAM, SHARD, 128), BF),
            dma((8,)), dma((8,)), dma((2,)), dma((8,)), dma((8,)), dma((2,)), dma((8,)), dma((8,)),
            dma((17,)), dma((16,)), dma((17,)), dma((16,)), dma((17,)), dma((16,)), dma((8,)), dma(()),
            dma((7, 16)), dma((7, 16)),
            dma((2, 4)), dma((2, 4)), dma((2, 4)), dma((2, 4)), dma((3, 4, 4)), dma((3, 4, 4)),
            dma((3, 2, 4)), dma((3, 2, 4)), dma((3, 16)), dma((3, 2, 8)), dma((8,)), dma((8,)), dma((4,)),
        ],
        compiler_params=pltpu.CompilerParams(
            collective_id=1, has_side_effects=True, vmem_limit_bytes=VMEM_BYTES
        ),
    )(feat, labels, table, order, neigh, counts, cot, wt)


def per_device(
    features, labels, label_table, proj_weight, block_order, neighbours, counts, cotangent
):
    wt = proj_weight.reshape(SHARD, 4, TEAM, 128).transpose(2, 0, 1, 3).reshape(TEAM, SHARD, 512)
    layer_out, features_grad, proj_grad = layer(
        features[0], labels, label_table, block_order, neighbours[0].T, counts, cotangent[0], wt
    )
    return (layer_out[None], features_grad[None], proj_grad)


def solution(mesh):
    placed = (
        P("dp", "seq", None),
        P("dp", "seq"),
        P(),
        P("seq", None, None),
        P("dp", None),
        P("dp", None, None),
        P("dp", None),
        P("dp", "seq", None),
    )
    return jax.shard_map(
        per_device,
        mesh=mesh,
        in_specs=placed,
        out_specs=(P("dp", "seq", None), P("dp", "seq", None), P("seq", None, None)),
        check_vma=False,
    )
```

```python
import jax
import jax.numpy as jnp
from jax import lax
from jax.experimental import pallas as pl
from jax.experimental.pallas import tpu as pltpu
from jax.sharding import PartitionSpec as P

XS, YS, TEAM, SEQ, ROWS, WIDTH = 4, 4, 8, 16, 128, 1024
SHARD = WIDTH // SEQ
HALF = 4 * ROWS
BF, F32 = jnp.bfloat16, jnp.float32
NN = (((1,), (0,)), ((), ()))
NT = (((1,), (1,)), ((), ()))
TN = (((0,), (0,)), ((), ()))
VMEM_BYTES = 40 << 20
MESH = pl.DeviceIdType.MESH
NEAR = (1, 3, 2)


def dot(a, b, dims=NN):
    return lax.dot_general(a, b, dims, preferred_element_type=F32)


def remote(src, dst, send, recv, where):
    return pltpu.make_async_remote_copy(
        src_ref=src, dst_ref=dst, send_sem=send, recv_sem=recv, device_id=where, device_id_type=MESH
    )


def push(src, dst, send, recv, where):
    copy = remote(src, dst, send, recv, where)
    copy.start()
    return copy


def arrival(dst, recv, where):
    remote(dst, dst, recv, recv, where).wait_recv()


def low_lanes(shape):
    return lax.broadcasted_iota(jnp.int32, shape, 1) < 64


def merge(a, b):
    return jnp.where(low_lanes(a.shape), a, pltpu.roll(b, 64, 1))


def merge_high(a, b):
    return jnp.where(low_lanes(a.shape), pltpu.roll(a, 64, 1), b)


def kernel(
    feat, labels, table, order, neigh, counts, cot, wt,
    layer_out, features_grad, proj_grad,
    hid, tab, hid8, cot8, hid_t, wg, wo, w_t, tab8, raw, slots_of, users_of, stage_qk, stage_v, stage_g, land_qk, land_v, land_g,
    v_full, probs, lows, tiles, back_a, back_q, back_k, back_v, home_a, home_q, home_k, home_v, mix,
    part, total, sib, far, terms_o, terms_q, terms_kv, from_y_o, from_y_q, from_y_kv,
    to_z_o, to_z_q, to_z_kv, from_z_o, from_z_q, from_z_kv, full_o, full_q, full_kv, wob,
    hid_s, hid_r, hid_h, cot_s, cot_r, cot_h, tab_s, tab_r, w_s, w_r, v_s, v_r, o_s, o_r, sc_s, sc_r,
    m_s, m_r, sib_s, sib_r, far_s, far_r, y_s, y_r, z_s, z_r, g_s, g_r, q_s, q_r, loc,
):
    dp, r = lax.axis_index("dp"), lax.axis_index("seq")
    zl, p = dp // TEAM, dp % TEAM
    x, c = p // 2, p % 2
    zh, y = r // YS, r % YS
    base = zl * TEAM
    me = c * XS + x
    sibling = (base + x * 2 + 1 - c, r)
    across = lax.rem(dp + TEAM, 2 * TEAM)

    def turn(k):
        return lax.rem(x + k, XS)

    def slot(k):
        return c * XS + turn(k)

    def at_x(k):
        return (base + turn(k) * 2 + c, r)

    def at_z(k):
        return lax.rem(zh + k, 4) * YS + y

    def at_y(k):
        return zh * YS + lax.rem(y + k, YS)

    def team_peer(k):
        return base + lax.rem(p + k, TEAM)

    def slot_of(q):
        return lax.rem(q, 2) * XS + q // 2

    barrier = pltpu.get_barrier_semaphore()
    greeted = [(lax.rem(dp + k, 2 * TEAM), r) for k in range(1, 2 * TEAM)]
    greeted += [(dp, lax.rem(r + k, SEQ)) for k in range(1, SEQ)]
    greeted += [(across, at_z(k)) for k in (1, 2, 3)]
    for where in greeted:
        pl.semaphore_signal(barrier, inc=1, device_id=where, device_id_type=MESH)
    chosen = lax.broadcasted_iota(jnp.int32, (table.shape[0], ROWS), 0) == labels[...]
    embedded = dot(chosen.astype(F32).astype(BF), table[...], TN)
    hid[...] = (feat[...].astype(F32) + embedded).astype(BF)
    tab[...] = jnp.zeros_like(tab)
    tab[0:1, 0:SEQ] = order[...]
    tab[1:2, 0:SEQ] = counts[...]
    tab[2:6, 0:SEQ] = neigh[...]
    pl.semaphore_wait(barrier, len(greeted))
    sends = []

    sources = (stage_qk, stage_v, stage_g, back_a, back_q, back_k, back_v)
    targets = (land_qk, land_v, land_g, home_a, home_q, home_k, home_v)

    def message(kind, t):
        return remote(
            sources[kind].at[t], targets[kind].at[r], m_s.at[kind, t], m_r.at[kind, r], (dp, t)
        )

    def after(k):
        return lax.rem(r + k, SEQ)

    def before(k):
        return lax.rem(r + SEQ - k, SEQ)

    def keep(kind):
        targets[kind][r] = sources[kind][r]

    def arrived(kind, t):
        arrival(targets[kind].at[t], m_r.at[kind, t], (dp, t))

    def give_group(kind, core):
        for n in range(TEAM):
            t = core * TEAM + n

            @pl.when(t != r)
            def _():
                message(kind, t).start()

            @pl.when(t == r)
            def _():
                keep(kind)

    def got_all(kind):
        def one(k, carry):
            arrived(kind, before(k))
            return carry

        lax.fori_loop(1, SEQ, one, 0)

    halves = (pl.ds(0, 64), pl.ds(64, 64))

    def spread_x(array, own, send, recv):
        for k in (1, 3):
            sends.append(push(own, array.at[me], send.at[k], recv.at[me], at_x(k)))
        sends.append(push(own, array.at[me], send.at[0], recv.at[me], sibling))

    def forward_x(array, send, recv, opposite):
        for k in (1, 3):
            q = slot(k)
            arrival(array.at[q], recv.at[q], at_x(k))
            h = k // 3
            piece = array.at[q, halves[h]]
            sends.append(push(piece, piece, send.at[4 + k], opposite.at[h], at_x(4 - k)))
            sends.append(push(array.at[q], array.at[q], send.at[1 + k], recv.at[q], sibling))

    def finish_x(array, send, recv, opposite):
        q = slot(2)
        for h, k in ((0, 1), (1, 3)):
            arrival(array.at[q, halves[h]], opposite.at[h], at_x(k))
        sends.append(push(array.at[q], array.at[q], send.at[6], recv.at[q], sibling))

    def other_core(array, recv):
        for k in range(XS):
            q = (1 - c) * XS + turn(k)
            arrival(array.at[q], recv.at[q], sibling)

    def rows_of(s):
        return pl.ds(pl.multiple_of(s * SHARD, SHARD), SHARD)

    def qk_part(s):
        return wg.at[rows_of(s), 0:256]

    def v_part(s):
        return wg.at[rows_of(s), 256:384]

    def out_part(s):
        return wg.at[rows_of(s), 384:512]

    own_w = pltpu.make_async_copy(wt.at[p, :, 0:384], wg.at[rows_of(r), 0:384], loc.at[0])
    own_w.start()
    mine_qk, mine_v = wt.at[p, :, 0:256], wt.at[p, :, 256:384]
    for k in NEAR:
        sends.append(push(mine_qk, qk_part(r), w_s.at[k], w_r.at[r], (dp, at_z(k))))
    for k in NEAR:
        sends.append(push(mine_qk, qk_part(r), w_s.at[3 + k], w_r.at[r], (dp, at_y(k))))
    for k in NEAR:
        sends.append(push(mine_v, v_part(r), v_s.at[k], v_r.at[r], (dp, at_z(k))))
    for k in NEAR:
        sends.append(push(mine_v, v_part(r), v_s.at[3 + k], v_r.at[r], (dp, at_y(k))))

    spread = r // 2 == p

    @pl.when(spread)
    def _():
        for j in range(TEAM):
            t = 2 * j + r % 2

            @pl.when(t != r)
            def _():
                push(wt.at[j, :, 384:512], out_part(t), sc_s.at[j], sc_r, (dp, t))

    keep_hid = pltpu.make_async_copy(hid, hid8.at[me], loc.at[1])
    keep_hid.start()
    keep_cot = pltpu.make_async_copy(cot, cot8.at[me], loc.at[2])
    keep_cot.start()
    spread_x(hid8, hid, hid_s, hid_r)
    for k in range(1, TEAM):
        sends.append(push(tab, tab8.at[me], tab_s.at[k], tab_r.at[me], (team_peer(k), r)))

    for n, k in enumerate(NEAR):
        s = at_z(k)
        arrival(qk_part(s), w_r.at[s], (dp, s))
        for m in NEAR:
            sends.append(
                push(qk_part(s), qk_part(s), w_s.at[7 + n * 3 + m], w_r.at[s], (dp, at_y(m)))
            )

    forward_x(hid8, hid_s, hid_r, hid_h)
    spread_x(cot8, cot, cot_s, cot_r)
    for n, k in enumerate(NEAR):
        s = at_z(k)
        arrival(v_part(s), v_r.at[s], (dp, s))
        for m in NEAR:
            sends.append(
                push(v_part(s), v_part(s), v_s.at[7 + n * 3 + m], v_r.at[s], (dp, at_y(m)))
            )

    piece = out_part(r)

    @pl.when(spread)
    def _():
        copy = pltpu.make_async_copy(wt.at[p, :, 384:512], piece, loc.at[3])
        copy.start()
        copy.wait()

    @pl.when(jnp.logical_not(spread))
    def _():
        arrival(piece, sc_r, (dp, r))

    for k in NEAR:
        sends.append(push(piece, piece, o_s.at[k], o_r.at[r], (dp, at_z(k))))
    for k in NEAR:
        sends.append(push(piece, piece, o_s.at[3 + k], o_r.at[r], (dp, at_y(k))))
    finish_x(hid8, hid_s, hid_r, hid_h)
    for n, k in enumerate(NEAR):
        s = at_z(k)
        arrival(out_part(s), o_r.at[s], (dp, s))
        for m in NEAR:
            sends.append(
                push(out_part(s), out_part(s), o_s.at[7 + n * 3 + m], o_r.at[s], (dp, at_y(m)))
            )

    def from_all_y(piece_of, sems):
        for m in NEAR:
            for k in range(4):
                s = lax.rem(zh + k, 4) * YS + lax.rem(y + m, YS)
                arrival(piece_of(s), sems.at[s], (dp, s))

    def group_rows(array, core):
        block = array[pl.ds(pl.multiple_of(core * XS, XS), XS)]
        return block.reshape(HALF, array.shape[2])

    def packed(stage, core, result):
        for n in range(XS):
            top = result[n * ROWS : n * ROWS + 64]
            bottom = result[n * ROWS + 64 : n * ROWS + ROWS]
            i = core * XS + n
            stage[2 * i] = merge(top, bottom)
            stage[2 * i + 1] = merge_high(top, bottom)

    from_all_y(qk_part, w_r)
    own_w.wait()
    keep_hid.wait()
    for core in (c, 1 - c):
        if core is not c:
            other_core(hid8, hid_r)
        queries_keys = dot(group_rows(hid8, core), wg[:, 0:256]).astype(BF)
        for n in range(XS):
            rows = queries_keys[n * ROWS : n * ROWS + ROWS]
            q, k = rows[:, 0:128], rows[:, 128:256]
            i = core * XS + n
            stage_qk[2 * i] = merge(q, k)
            stage_qk[2 * i + 1] = merge_high(q, k)
        give_group(0, core)

    forward_x(cot8, cot_s, cot_r, cot_h)
    from_all_y(v_part, v_r)
    for core in (c, 1 - c):
        packed(stage_v, core, dot(group_rows(hid8, core), wg[:, 256:384]).astype(BF))
        give_group(1, core)
    from_all_y(out_part, o_r)
    for j in range(TEAM):
        block = wg[128 * j : 128 * j + 128, 384:512]
        wo[128 * j : 128 * j + 128, :] = block.T
        w_t[384:512, 128 * j : 128 * j + 128] = block
    finish_x(cot8, cot_s, cot_r, cot_h)
    keep_cot.wait()
    for core in (c, 1 - c):
        if core is not c:
            other_core(cot8, cot_r)
        packed(stage_g, core, dot(group_rows(cot8, core), wo[...]).astype(BF))
        give_group(2, core)


    for n in range(3):
        w_t[128 * n : 128 * n + 128, :] = wg[:, 128 * n : 128 * n + 128].T
    for q in range(TEAM):
        hid_t[:, 128 * q : 128 * q + 128] = hid8[q].T

    for k in range(1, TEAM):
        i = lax.rem(p + k, TEAM)
        q = slot_of(i)
        arrival(tab8.at[q], tab_r.at[q], (base + i, r))
    tab8[me] = tab[...]
    to_scalars = pltpu.make_async_copy(tab8.at[r // 2], raw, loc.at[3])
    to_scalars.start()
    to_scalars.wait()

    def list_blocks(s, carry):
        for b in range(SEQ):
            users_of[b, s] = 64
        for j in range(4):
            name = raw[2 + j, s]
            found = 0
            for b in range(SEQ):
                hit = raw[0, b] == name
                found = jnp.where(hit, b, found)
                users_of[b, s] = jnp.where(hit, 4 * s + j, users_of[b, s])
            slots_of[s, j] = found
        return carry

    lax.fori_loop(0, SEQ, list_blocks, 0)

    lo = low_lanes((128, 128))
    zero = jnp.zeros((128, 128), BF)
    got_all(0)

    def probabilities(s):
        qz = jnp.where(lo, zero, pltpu.roll(land_qk[s], 64, 1)) * jnp.asarray(0.125, BF)
        count = raw[1, s]
        scores = [
            jnp.where(j < count, dot(land_qk[slots_of[s, j]], qz, NT), -1e30) for j in range(4)
        ]
        top = jnp.max(
            jnp.maximum(jnp.maximum(scores[0], scores[1]), jnp.maximum(scores[2], scores[3])),
            axis=0,
            keepdims=True,
        )
        expo = [jnp.exp(v - top) for v in scores]
        total = jnp.sum((expo[0] + expo[1]) + (expo[2] + expo[3]), axis=0, keepdims=True)
        inv = 1.0 / total
        for j in range(4):
            prob = expo[j] * inv
            probs[s, j] = prob
            lows[s, 128 * j : 128 * j + 128] = prob.astype(BF)

    def forward(g, carry):
        for n in range(4):
            probabilities(4 * g + n)
        return carry

    lax.fori_loop(0, 4, forward, 0)
    got_all(1)
    for s in range(SEQ):
        v_full[s, 0:64] = land_v[s]
        v_full[s, 64:128] = pltpu.roll(land_v[s], 64, 1)

    def blocks_of(g):
        return [lax.rem(r + 1 + 4 * g + n, SEQ) for n in range(4)]

    def hand_over(kind, g):
        for n, s in enumerate(blocks_of(g)):
            if n < 3:
                message(kind, s).start()
            else:

                @pl.when(s != r)
                def _():
                    message(kind, s).start()

    def attention(g, carry):
        for s in blocks_of(g):
            values = [v_full[slots_of[s, j]] for j in range(4)]
            attn = dot(jnp.concatenate(values, axis=0), lows[s], TN).T.astype(BF)
            back_a[s] = merge(attn[0:64], attn[64:128])
        hand_over(3, g)
        return carry

    lax.fori_loop(0, 4, attention, 0)
    keep(3)
    got_all(2)

    def gradients(s):
        qk, grad = land_qk[s], land_g[s]
        turned = pltpu.roll(grad, 64, 1)
        gz = jnp.where(lo, jnp.concatenate([grad, turned], axis=0), zero)
        gv = jnp.where(lo, zero, jnp.concatenate([turned, grad], axis=0))
        rhs = jnp.concatenate([jnp.where(lo, qk, zero), gv], axis=0)
        slots = [slots_of[s, j] for j in range(4)]
        keys = [land_qk[b] for b in slots]
        grad_p = [dot(v_full[b], gz, NT) for b in slots]
        prob = [probs[s, j] for j in range(4)]
        prod = [a * g for a, g in zip(prob, grad_p)]
        delta = jnp.sum((prod[0] + prod[1]) + (prod[2] + prod[3]), axis=0, keepdims=True)
        grad_s = [(a * (g - delta) * 0.125).astype(BF) for a, g in zip(prob, grad_p)]
        grad_q = dot(
            jnp.concatenate(keys, axis=0), jnp.concatenate(grad_s, axis=0), TN
        ).T.astype(BF)
        back_q[s] = merge_high(grad_q[0:64], grad_q[64:128])
        for j in range(4):
            low = lows[s, 128 * j : 128 * j + 128]
            tiles[4 * s + j] = dot(jnp.concatenate([grad_s[j], low], axis=1), rhs)

    def backward(g, carry):
        for s in blocks_of(g):
            gradients(s)
        hand_over(4, g)
        return carry

    lax.fori_loop(0, 4, backward, 0)
    keep(4)
    tiles[64] = jnp.zeros((128, 128), F32)

    def collect(n, carry):
        b = lax.rem(r + 1 + n, SEQ)
        total = tiles[users_of[b, 0]]
        for s in range(1, SEQ):
            total += tiles[users_of[b, s]]
        low = total.astype(BF)
        back_k[b] = merge(low[0:64], low[64:128])
        back_v[b] = merge_high(low[0:64], low[64:128])

        @pl.when(n < SEQ - 1)
        def _():
            message(5, b).start()
            message(6, b).start()

        return carry

    lax.fori_loop(0, SEQ, collect, 0)
    keep(5)
    keep(6)

    def half_rows(core):
        return pl.ds(pl.multiple_of(core * HALF, HALF), HALF)

    def take(core, kind):
        for n in range(XS):
            i = core * XS + n
            a, b = targets[kind][2 * i], targets[kind][2 * i + 1]
            start = pl.multiple_of(i * ROWS, ROWS)
            cols = pl.ds(128 * (kind - 3), 128)
            mix[pl.ds(start, 64), cols] = merge(a, b)
            mix[pl.ds(start + 64, 64), cols] = merge_high(a, b)

    def product(core, n):
        if n == 0:
            return dot(mix[half_rows(core), 0:128], w_t[384:512, :])
        return dot(mix[half_rows(core), 128:512], w_t[0:384, :])

    def share(n):
        result = product(1 - c, n).astype(BF)
        for i in range(XS):
            part[n, i] = result[i * ROWS : i * ROWS + ROWS]
        for k in (1, 3, 2, 0):
            i = turn(k)
            sends.append(push(part.at[n, i], sib.at[n, i], sib_s.at[n, k], sib_r.at[n, i], sibling))

    def pass_on(n):
        result = product(c, n)
        for i in range(XS):
            total[i] = result[i * ROWS : i * ROWS + ROWS]
        for k in (1, 3, 2, 0):
            i = turn(k)
            arrival(sib.at[n, i], sib_r.at[n, i], sibling)
            part[n, XS + i] = (total[i] + sib[n, i].astype(F32)).astype(BF)
            if k:
                sends.append(
                    push(part.at[n, XS + i], far.at[n, x], far_s.at[n, k], far_r.at[n, x], at_x(k))
                )

    def result_of(n, first):
        result = first.astype(F32) + part[n, XS + x].astype(F32)
        for k in NEAR:
            arrival(far.at[n, turn(k)], far_r.at[n, turn(k)], at_x(k))
            result += far[n, turn(k)].astype(F32)
        return result.astype(BF)

    terms = (terms_o, terms_q, terms_kv)
    from_y = (from_y_o, from_y_q, from_y_kv)
    to_z = (to_z_o, to_z_q, to_z_kv)
    from_z = (from_z_o, from_z_q, from_z_kv)
    full = (full_o, full_q, full_kv)

    def terms_out(g):
        if g == 0:
            cots = cot8[...].reshape(TEAM * ROWS, WIDTH)
            out_term = dot(mix[:, 0:128], cots, TN).astype(BF)
            for j in range(TEAM):
                block = out_term[:, 128 * j : 128 * j + 128]
                terms_o[2 * j] = block[0:64]
                terms_o[2 * j + 1] = block[64:128]
        for h in range(4):
            if g:
                cols = mix[:, 128 * g : 256 * g]
                in_term = dot(hid_t[256 * h : 256 * h + 256], cols).astype(BF)
                for m in range(YS):
                    terms[g][4 * h + m] = in_term[64 * m : 64 * m + 64]
            for k in NEAR:
                sends.append(
                    push(
                        terms[g].at[4 * h + lax.rem(y + k, YS)], from_y[g].at[y, h],
                        y_s.at[g, k, h], y_r.at[g, y, h], (dp, at_y(k)),
                    )
                )

    def half_of(side):
        return pl.ds(pl.multiple_of(side * 32, 32), 32)

    def along_z(g):
        for k in (2, 1, 3, 0):
            h = lax.rem(zh + k, 4)
            result = terms[g][4 * h + y].astype(F32)
            for m in NEAR:
                t = lax.rem(y + m, YS)
                arrival(from_y[g].at[t, h], y_r.at[g, t, h], (dp, at_y(m)))
                result += from_y[g][t, h].astype(F32)
            to_z[g][h] = result.astype(BF)
            for other in (0, 1):
                if k or other:
                    side = lax.rem(zl + other, 2)
                    where = across if other else dp
                    sends.append(
                        push(
                            to_z[g].at[h, half_of(side)], from_z[g].at[zl, zh],
                            z_s.at[g, other, h], z_r.at[g, zl, zh], (where, h * YS + y),
                        )
                    )

    def to_team(g):
        result = to_z[g][zh, half_of(zl)].astype(F32)
        for k in (1, 3, 2, 0):
            h = lax.rem(zh + k, 4)
            for other in (0, 1):
                if k or other:
                    side = lax.rem(zl + other, 2)
                    arrival(from_z[g].at[side, h], z_r.at[g, side, h], (dp, at_z(k)))
                    result += from_z[g][side, h].astype(F32)
        piece = full[g].at[me, half_of(zl)]
        piece[...] = result.astype(BF)
        for k in range(1, 2 * TEAM):
            where = lax.rem(dp + k, 2 * TEAM)
            sends.append(push(piece, piece, g_s.at[g, k], g_r.at[g, zl, me], (where, r)))

    def from_team(g):
        for k in range(1, 2 * TEAM):
            other = lax.rem(dp + k, 2 * TEAM)
            side, q = other // TEAM, slot_of(other % TEAM)
            arrival(full[g].at[q, half_of(side)], g_r.at[g, side, q], (other, r))

    def out_piece(i):
        t = 2 * i + r % 2
        src = full_o.at[(i % 2) * XS + i // 2]
        return t, remote(src, wob.at[r // 2], q_s.at[i], q_r.at[r // 2], (dp, t))

    def write(n, source, first):
        for i in range(TEAM):
            q = (i % 2) * XS + i // 2
            piece = source[q, :, first : first + 128]
            proj_grad[:, n, 128 * i : 128 * i + 128] = piece.astype(F32)

    def take_all(kind):
        take(0, kind)
        take(1, kind)

    got_all(3)
    take_all(3)
    share(0)
    terms_out(0)
    pass_on(0)
    got_all(4)
    take_all(4)
    terms_out(1)
    along_z(0)
    got_all(5)
    take_all(5)
    got_all(6)
    take_all(6)
    terms_out(2)
    share(1)
    to_team(0)
    along_z(1)
    pass_on(1)
    from_team(0)
    for i in range(TEAM):
        t, copy = out_piece(i)

        @pl.when(t != r)
        def _():
            copy.start()

        @pl.when(t == r)
        def _():
            wob[r // 2] = full_o[(i % 2) * XS + i // 2]

    to_team(1)
    along_z(2)
    layer_out[...] = result_of(0, hid8[me])
    from_team(1)
    write(0, full_q, 0)
    for j in range(TEAM):
        t, copy = out_piece(j)

        @pl.when(t != r)
        def _():
            arrival(wob.at[j], q_r.at[j], (dp, t))
            copy.wait_send()

        proj_grad[:, 3, 128 * j : 128 * j + 128] = wob[j].astype(F32)
    to_team(2)
    features_grad[...] = result_of(1, cot8[me])
    from_team(2)
    write(1, full_kv, 0)
    write(2, full_kv, 128)

    for copy in sends:
        copy.wait_send()

    @pl.when(spread)
    def _():
        for j in range(TEAM):
            t = 2 * j + r % 2

            @pl.when(t != r)
            def _():
                remote(
                    wt.at[j, :, 384:512], out_part(t), sc_s.at[j], sc_r, (dp, t)
                ).wait_send()

    def sent(k, carry):
        t = lax.rem(r + k, SEQ)
        for kind in range(7):
            message(kind, t).wait_send()
        return carry

    lax.fori_loop(1, SEQ, sent, 0)


def layer(feat, labels, table, order, neigh, counts, cot, wt):
    vmem = pl.BlockSpec(memory_space=pltpu.VMEM)
    dma = pltpu.SemaphoreType.DMA
    tile, small = (128, 128), (64, 128)
    act = (ROWS, WIDTH)
    widths = (128, 128, 256)
    return pl.pallas_call(
        kernel,
        out_shape=[
            jax.ShapeDtypeStruct(act, BF),
            jax.ShapeDtypeStruct(act, BF),
            jax.ShapeDtypeStruct((SHARD, 4, WIDTH), F32),
        ],
        in_specs=[vmem] * 6 + [pl.BlockSpec(memory_space=pl.ANY), vmem],
        out_specs=[vmem] * 3,
        scratch_shapes=[
            pltpu.VMEM(act, BF),
            pltpu.VMEM((8, 128), jnp.int32),
            pltpu.VMEM((TEAM, *act), BF),
            pltpu.VMEM((TEAM, *act), BF),
            pltpu.VMEM((WIDTH, TEAM * ROWS), BF),
            pltpu.VMEM((WIDTH, 512), BF),
            pltpu.VMEM((WIDTH, 128), BF),
            pltpu.VMEM((512, WIDTH), BF),
            pltpu.VMEM((TEAM, 8, 128), jnp.int32),
            pltpu.SMEM((8, 128), jnp.int32),
            pltpu.SMEM((SEQ, 4), jnp.int32),
            pltpu.SMEM((SEQ, SEQ), jnp.int32),
            pltpu.VMEM((SEQ, *tile), BF),
            pltpu.VMEM((SEQ, *small), BF),
            pltpu.VMEM((SEQ, *small), BF),
            pltpu.VMEM((SEQ, *tile), BF),
            pltpu.VMEM((SEQ, *small), BF),
            pltpu.VMEM((SEQ, *small), BF),
            pltpu.VMEM((SEQ, *tile), BF),
            pltpu.VMEM((SEQ, 4, *tile), F32),
            pltpu.VMEM((SEQ, 512, 128), BF),
            pltpu.VMEM((SEQ * 4 + 1, *tile), F32),
            *[pltpu.VMEM((SEQ, *small), BF)] * 8,
            pltpu.VMEM((TEAM * ROWS, 512), BF),
            pltpu.VMEM((2, 2 * XS, *act), BF),
            pltpu.VMEM((XS, *act), F32),
            pltpu.VMEM((2, XS, *act), BF),
            pltpu.VMEM((2, XS, *act), BF),
            *[pltpu.VMEM((SEQ, SHARD, w), BF) for w in widths],
            *[pltpu.VMEM((YS, 4, SHARD, w), BF) for w in widths],
            *[pltpu.VMEM((4, SHARD, w), BF) for w in widths],
            *[pltpu.VMEM((2, 4, SHARD // 2, w), BF) for w in widths],
            *[pltpu.VMEM((TEAM, SHARD, w), BF) for w in widths],
            pltpu.VMEM((TEAM, SHARD, 128), BF),
            dma((8,)), dma((8,)), dma((2,)), dma((8,)), dma((8,)), dma((2,)), dma((8,)), dma((8,)),
            dma((17,)), dma((16,)), dma((17,)), dma((16,)), dma((17,)), dma((16,)), dma((8,)), dma(()),
            dma((7, 16)), dma((7, 16)),
            dma((2, 4)), dma((2, 4)), dma((2, 4)), dma((2, 4)), dma((3, 4, 4)), dma((3, 4, 4)),
            dma((3, 2, 4)), dma((3, 2, 4)), dma((3, 16)), dma((3, 2, 8)), dma((8,)), dma((8,)), dma((4,)),
        ],
        compiler_params=pltpu.CompilerParams(
            collective_id=1, has_side_effects=True, vmem_limit_bytes=VMEM_BYTES
        ),
    )(feat, labels, table, order, neigh, counts, cot, wt)


def per_device(
    features, labels, label_table, proj_weight, block_order, neighbours, counts, cotangent
):
    wt = proj_weight.reshape(SHARD, 4, TEAM, 128).transpose(2, 0, 1, 3).reshape(TEAM, SHARD, 512)
    layer_out, features_grad, proj_grad = layer(
        features[0], labels, label_table, block_order, neighbours[0].T, counts, cotangent[0], wt
    )
    return (layer_out[None], features_grad[None], proj_grad)


def solution(mesh):
    placed = (
        P("dp", "seq", None),
        P("dp", "seq"),
        P(),
        P("seq", None, None),
        P("dp", None),
        P("dp", None, None),
        P("dp", None),
        P("dp", "seq", None),
    )
    return jax.shard_map(
        per_device,
        mesh=mesh,
        in_specs=placed,
        out_specs=(P("dp", "seq", None), P("dp", "seq", None), P("seq", None, None)),
        check_vma=False,
    )
```
